512 devices in a mesh: tile: 16 (over y, x), fsdp: 32 (over z, core).
Axes of the slice: x: 4, y: 4, z: 16, core: 2. Of those that a mesh axis runs over, the one named last changes fastest.
Arguments:
- images: bfloat16 [32, 64, 64, 2048], P('fsdp', 'tile'), may hold values from -80 to 80
- w_qkv: bfloat16 [2048, 3072], P(None, ('tile', 'fsdp')), may hold values from -0.125 to 0.125
- prev_scale: float32 [1], replicated, may hold values from 0.06 to 0.11
- extent: int32 [32, 2], P('fsdp'), may hold values from 32 to 64, as said below
Outputs:
- attended: bfloat16 [32, 64, 64, 1024], P('fsdp', 'tile')
- new_scales: float32 [2], replicated
The draws below stay inside these ranges and needn't reach their ends.
Inputs may be any that keep to these rules, and one draw needn't show every extreme that they name: `extent`: each image's valid tokens are its top-left rows (first entry) and columns (second entry), at least half of each; image 0 is whole.
All inputs are finite; a program needn't handle non-finite values.
Results may differ from the reference program's by a relative error of at most 0.01.
The reference program's roundings to bfloat16 on the way (of `quantized`, `qkv` and `probabilities`) count: a program that leaves them out, or rounds other values in their place, can miss the bound.
Values may be sent and summed in bfloat16 or wider, within the bound.
No kernel may reach another device: no remote copies, remote signals or barrier semaphores. Data moves between devices by JAX's collectives and lax.ppermute only.
A program may use at most 128 MiB of HBM per device.

```python
import math
import jax
import jax.numpy as jnp
from jax import lax

D = 2048
HEADS = 8
HEAD = 128
COLS = 64
IMAGES = 32
HT = 64


def draw_images(key, part):
    key = jax.random.fold_in(key, 11)
    key_noise, key_scale = jax.random.split(key, 2)
    shape = (IMAGES, HT, COLS, D)
    ramp = 1.0 + 2.0 * jnp.arange(HT, dtype=jnp.float32) / (HT - 1)
    noise = jax.random.truncated_normal(key_noise, -6.0, 6.0, shape, jnp.float32)
    spread = jnp.log(4.0)
    row_scale = jnp.exp(jax.random.uniform(key_scale, (IMAGES, HT, 1, 1), jnp.float32, 0.0, 1.0) * spread)
    return (noise * row_scale * ramp[None, :, None, None]).astype(jnp.bfloat16)


def draw_extent(key, part):
    key = jax.random.fold_in(key, 12)
    key_rows, key_cols = jax.random.split(key, 2)
    valid_rows = jax.random.randint(key_rows, (IMAGES,), HT // 2, HT + 1).at[0].set(HT)
    valid_cols = jax.random.randint(key_cols, (IMAGES,), COLS // 2, COLS + 1).at[0].set(COLS)
    return jnp.stack([valid_rows, valid_cols], axis=1).astype(jnp.int32)


def levels(rng, dims, cuts, smallest, high):
    level, own = 1.0, jax.random.fold_in(rng, 6)
    for dim, shards_of in cuts:
        heights = jnp.exp(jax.random.uniform(jax.random.fold_in(own, dim), (shards_of,), jnp.float32, smallest / len(cuts), high / len(cuts)))
        level = level * jnp.repeat(heights, dims[dim] // shards_of).reshape([-1 if axis == dim else 1 for axis in range(len(dims))])
    return level


def bell_draw(key, dims, scale, limit, cuts=(), kind=jnp.bfloat16):
    array = jax.random.normal(key, dims, jnp.float32) * scale
    if len(cuts) > 0:
        array = levels(key, dims, cuts, -0.22, 0.18) * array
    return jnp.clip(array, min=-limit, max=limit).astype(kind)


def setup_inputs(seed: int = 0) -> dict:
    key_list = jax.random.split(jax.random.key(seed), 5)
    images = draw_images(jax.random.fold_in(key_list[4], 71), 0)
    w_qkv = bell_draw(key_list[1], (D, 3 * HEADS * HEAD), D ** -0.5, 0.125, ((1, 512),))
    prev_scale = jnp.clip(jnp.exp(jax.random.uniform(key_list[2], (1,), jnp.float32, math.log(0.06), math.log(0.11))), 0.06, 0.11)
    extent = draw_extent(jax.random.fold_in(key_list[4], 71), 0)
    return dict(images=images, w_qkv=w_qkv, prev_scale=prev_scale, extent=extent)


half_window = 3
fp_top = 448.0


def neighbourhood(query, keys, values, row_start, ext_rows, ext_cols):
    row_count, col_count, head_count, head_size = query.shape
    scaling = float(head_size) ** -0.5
    query_wide = query.astype(jnp.float32)
    row_ids = row_start + jnp.arange(row_count, dtype=jnp.int32)
    col_ids = jnp.arange(col_count, dtype=jnp.int32)
    scores = []
    allowed = []
    for row_shift in range(2 * half_window + 1):
        for col_shift in range(2 * half_window + 1):
            key_part = keys[row_shift:row_shift + row_count, col_shift:col_shift + col_count].astype(jnp.float32)
            scores.append(jnp.sum(query_wide * key_part, axis=-1) * scaling)
            key_rows = row_ids + (row_shift - half_window)
            key_cols = col_ids + (col_shift - half_window)
            inside = ((key_rows >= 0) & (key_rows < ext_rows))[:, None] & ((key_cols >= 0) & (key_cols < ext_cols))[None, :]
            if row_shift == half_window and col_shift == half_window:
                inside = jnp.ones_like(inside)
            allowed.append(inside)
    scores = jnp.stack(scores)
    allowed = jnp.stack(allowed)[..., None]
    highest = jnp.max(jnp.where(allowed, scores, -1e30), axis=0)
    weights = jnp.where(allowed, jnp.exp(scores - highest), 0.0)
    denominator = jnp.sum(weights, axis=0)
    probabilities = (weights / denominator).astype(jnp.bfloat16)
    attended = jnp.zeros(query.shape, jnp.float32)
    position = 0
    for row_shift in range(2 * half_window + 1):
        for col_shift in range(2 * half_window + 1):
            value_part = values[row_shift:row_shift + row_count, col_shift:col_shift + col_count].astype(jnp.float32)
            attended = attended + probabilities[position].astype(jnp.float32)[..., None] * value_part
            position = position + 1
    query_valid = (row_ids < ext_rows)[:, None] & (col_ids < ext_cols)[None, :]
    attended = jnp.where(query_valid[:, :, None, None], attended, 0.0)
    return attended.astype(jnp.bfloat16).reshape(row_count, col_count, head_count * head_size)


def reference(images, w_qkv, prev_scale, extent):
    scale_prev = prev_scale[0]

    def per_image(inputs):
        one_image, bounds = inputs
        quantized = jnp.clip(one_image.astype(jnp.float32) / scale_prev, -fp_top, fp_top).astype(jnp.bfloat16)
        qkv = (jnp.dot(quantized.reshape(-1, D), w_qkv, preferred_element_type=jnp.float32) * scale_prev).astype(jnp.bfloat16)
        qkv = qkv.reshape(HT, COLS, 3, HEADS, HEAD)
        padding = ((half_window, half_window), (half_window, half_window), (0, 0), (0, 0))
        keys = jnp.pad(qkv[:, :, 1], padding)
        values = jnp.pad(qkv[:, :, 2], padding)
        return neighbourhood(qkv[:, :, 0], keys, values, jnp.int32(0), bounds[0], bounds[1])

    attended = lax.map(per_image, (images, extent))
    peak_in = jnp.max(jnp.abs(images.astype(jnp.float32)))
    peak_out = jnp.max(jnp.abs(attended.astype(jnp.float32)))
    return attended, jnp.stack([peak_in, peak_out]) / fp_top
```

```python
import functools

import jax
import jax.numpy as jnp
from jax import lax
from jax.experimental import pallas as pl
from jax.experimental.pallas import tpu as pltpu
from jax.sharding import Mesh
from jax.sharding import PartitionSpec as P

HEADS = 8
HEAD = 128
D = 2048
COLS = 64
ROWS = 4
HALO = 3
BLOCK = 16
SET = ROWS * COLS
KV_ROWS = (BLOCK + 2 * HALO) * COLS
FP_TOP = 448.0
AXES = ("y", "x", "z", "core")
GROUP = ("x", "core")
PEAK_ROWS = 16
NEG = -1e30


def device_of(y, x, z, core):
    return ((y * 4 + x) * 16 + z) * 2 + core


def head_permutations():
    main, extra = [], []
    for tile in range(16):
        m, odd = divmod(tile, 2)
        for shard in range(32):
            z, core = divmod(shard, 2)
            source = tile * 32 + shard
            cut = 10 if odd else 21
            first = 3 * m + odd

            def target(block):
                head = block % HEADS
                return device_of(2 * odd + core, head // 2, z, head % 2)

            main.append((source, target(first if shard <= cut else first + 1)))
            if shard == cut:
                extra.append((source, target(first + 1)))
    return main, extra


def column_order(head):
    d = lax.broadcasted_iota(jnp.int32, (3 * HEAD, 3 * HEAD), 1)
    r = lax.broadcasted_iota(jnp.int32, (3 * HEAD, 3 * HEAD), 0)
    natural = ((head + 2 * (d // HEAD)) % 3) * HEAD + d % HEAD
    half, m = natural // 192, natural % 192
    z, core, j = m // 12, (m % 12) // 6, m % 6
    return ((2 * half + core) * 96 + z * 6 + j == r).astype(jnp.bfloat16)


def project_kernel(scale_ref, x_ref, w_ref, order_ref, qkv_ref, top_ref, bottom_ref, w_scr):
    step = pl.program_id(0)

    @pl.when(step == 0)
    def _():
        w_scr[...] = lax.dot_general(
            w_ref[...], order_ref[...], (((0,), (0,)), ((), ())), preferred_element_type=jnp.float32
        ).astype(jnp.bfloat16)

    out = jnp.dot(x_ref[0], w_scr[...], preferred_element_type=jnp.float32) * scale_ref[0]
    out = out.astype(jnp.bfloat16)
    qkv_ref[0] = out
    for core in range(2):

        @pl.when(step == core)
        def _():
            top_ref[core] = out[: HALO * COLS, HEAD:]

        @pl.when(step == 6 + core)
        def _():
            bottom_ref[core] = out[SET - HALO * COLS :, HEAD:]


def project(scale, tokens, weights, order):
    halo = jax.ShapeDtypeStruct((2, HALO * COLS, 2 * HEAD), jnp.bfloat16)
    whole = lambda *shape: pl.BlockSpec(shape, lambda g: (0,) * len(shape))
    return pl.pallas_call(
        project_kernel,
        grid=(8,),
        out_shape=(jax.ShapeDtypeStruct((8, SET, 3 * HEAD), jnp.bfloat16), halo, halo),
        in_specs=[
            pl.BlockSpec(memory_space=pltpu.SMEM),
            pl.BlockSpec((1, SET, D), lambda g: (g, 0, 0)),
            whole(3 * HEAD, D),
            whole(3 * HEAD, 3 * HEAD),
        ],
        out_specs=(
            pl.BlockSpec((1, SET, 3 * HEAD), lambda g: (g, 0, 0)),
            whole(2, HALO * COLS, 2 * HEAD),
            whole(2, HALO * COLS, 2 * HEAD),
        ),
        scratch_shapes=[pltpu.VMEM((D, 3 * HEAD), jnp.bfloat16)],
        compiler_params=pltpu.CompilerParams(vmem_limit_bytes=40 * 2**20),
        cost_estimate=pl.CostEstimate(
            flops=2 * 8 * SET * D * 3 * HEAD, bytes_accessed=12 * 2**20, transcendentals=0
        ),
        name="project",
    )(scale, tokens, weights, order)


def attend_kernel(place_ref, peak_ref, qkv_ref, above_ref, below_ref, out_ref, kv):
    base = place_ref[0]
    scaling = float(HEAD) ** -0.5
    shape = (2 * COLS, 8 * COLS)
    q_row = lax.broadcasted_iota(jnp.int32, shape, 0)
    k_row = lax.broadcasted_iota(jnp.int32, shape, 1)
    row_step = k_row // COLS - q_row // COLS
    col_step = k_row % COLS - q_row % COLS
    window = (row_step >= 0) & (row_step <= 2 * HALO) & (col_step >= -HALO) & (col_step <= HALO)
    window = jnp.where(window, 0.0, NEG)
    centre = jnp.where((row_step == HALO) & (col_step == 0), 0.0, NEG)
    key_at = lax.broadcasted_iota(jnp.int32, (1, 8 * COLS), 1)
    query_at = lax.broadcasted_iota(jnp.int32, (2 * COLS, 1), 0)
    highest = jnp.zeros((2 * COLS, HEAD), jnp.float32)
    for image in range(2):
        ext_rows, ext_cols = place_ref[1 + 2 * image], place_ref[2 + 2 * image]
        kv[image, : HALO * COLS] = above_ref[image]
        for part in range(4):
            start = HALO * COLS + part * SET
            kv[image, start : start + SET] = qkv_ref[2 * part + image, :, HEAD:]
        kv[image, KV_ROWS - HALO * COLS :] = below_ref[image]
        for pair in range(BLOCK // 2):
            group, inner = 2 * (pair // 2) + image, (pair % 2) * 2 * COLS
            query = qkv_ref[group, inner : inner + 2 * COLS, :HEAD]
            start = 2 * pair * COLS
            keys = kv[image, start : start + 8 * COLS, :HEAD]
            values = kv[image, start : start + 8 * COLS, HEAD:]
            scores = lax.dot_general(
                query, keys, (((1,), (1,)), ((), ())), preferred_element_type=jnp.float32
            )
            key_rows = base + (2 * pair - HALO) + key_at // COLS
            key_cols = key_at % COLS
            valid = (key_rows >= 0) & (key_rows < ext_rows) & (key_cols < ext_cols)
            bias = jnp.maximum(jnp.where(valid, 0.0, NEG), centre) + window
            scores = scores * scaling + bias
            weights = jnp.exp(scores - jnp.max(scores, axis=1, keepdims=True))
            weights = weights * (1.0 / jnp.sum(weights, axis=1, keepdims=True))
            result = jnp.dot(
                weights.astype(jnp.bfloat16), values, preferred_element_type=jnp.float32
            )
            inside = (base + 2 * pair + query_at // COLS < ext_rows) & (query_at % COLS < ext_cols)
            result = jnp.where(inside, result, 0.0)
            highest = jnp.maximum(highest, jnp.abs(result))
            out_ref[group, inner : inner + 2 * COLS, :] = result.astype(jnp.bfloat16)
    peak_out = jnp.max(highest, axis=0, keepdims=True)
    lines = lax.broadcasted_iota(jnp.int32, (PEAK_ROWS, HEAD), 0)
    peaks = jnp.where(lines < PEAK_ROWS // 2, peak_out, peak_ref[0]).astype(jnp.bfloat16)
    for group in range(8):
        out_ref[group, SET:, :] = peaks


def attend(place, peak_in, qkv, above, below):
    vmem = pl.BlockSpec(memory_space=pltpu.VMEM)
    smem = pl.BlockSpec(memory_space=pltpu.SMEM)
    return pl.pallas_call(
        attend_kernel,
        out_shape=jax.ShapeDtypeStruct((8, SET + PEAK_ROWS, HEAD), jnp.bfloat16),
        in_specs=[smem, smem, vmem, vmem, vmem],
        out_specs=vmem,
        scratch_shapes=[pltpu.VMEM((2, KV_ROWS, 2 * HEAD), jnp.bfloat16)],
        compiler_params=pltpu.CompilerParams(vmem_limit_bytes=40 * 2**20),
        cost_estimate=pl.CostEstimate(
            flops=4 * 16 * 128 * 512 * HEAD, bytes_accessed=3 * 2**20, transcendentals=16 * 128 * 512
        ),
        name="attend",
    )(place, peak_in, qkv, above, below)


def spread(value, axis):
    size = lax.axis_size(axis)
    copies = jnp.broadcast_to(value[None], (size,) + value.shape)
    return lax.all_to_all(copies, axis, 0, 0, tiled=True)


def head_weights(w_qkv):
    main, extra = head_permutations()
    mine = w_qkv.T
    first = lax.ppermute(mine, AXES, main)
    second = lax.ppermute(mine, AXES, extra)
    y, z = lax.axis_index("y"), lax.axis_index("z")
    shard = 2 * z + y % 2
    cut = jnp.where((y < 2) & (shard == 21), 2, jnp.where((y >= 2) & (shard == 10), 4, 6))
    column = lax.broadcasted_iota(jnp.int32, mine.shape, 0)
    merged = jnp.where(column < cut, first, second)
    with jax.named_scope("weights_over_z"):
        over_z = spread(merged.reshape(96, 128), "z").reshape(96, D)
    with jax.named_scope("weights_over_y"):
        return spread(over_z, "y").reshape(3 * HEAD, D)


def local(images, w_qkv, prev_scale, extent):
    flat = images.reshape(SET, D).astype(jnp.float32)
    quantized = jnp.clip(flat / prev_scale[0], -FP_TOP, FP_TOP).astype(jnp.bfloat16)
    peak_in = jnp.max(jnp.abs(flat)).reshape(1)
    with jax.named_scope("tokens"):
        tokens = lax.all_gather(quantized, GROUP, axis=0, tiled=False)
    weights = head_weights(w_qkv)
    core = lax.axis_index("core")
    order = column_order(2 * lax.axis_index("x") + core)
    other = lax.ppermute(extent, "core", [(0, 1), (1, 0)])
    extents = jnp.where(core == 0, jnp.concatenate([extent, other]), jnp.concatenate([other, extent]))
    place = jnp.concatenate([(lax.axis_index("y") * BLOCK).reshape(1), extents.reshape(4)])
    qkv, top, bottom = project(prev_scale, tokens, weights, order)
    with jax.named_scope("halo"):
        above = lax.ppermute(bottom, "y", [(i, i + 1) for i in range(3)])
        below = lax.ppermute(top, "y", [(i + 1, i) for i in range(3)])
    mixed = attend(place.astype(jnp.int32), peak_in, qkv, above, below)
    with jax.named_scope("heads"):
        mixed = lax.all_to_all(mixed, GROUP, 0, 0, tiled=True)
    attended = mixed[:, :SET].transpose(1, 0, 2).reshape(1, ROWS, COLS, HEADS * HEAD)
    peaks = mixed[:, SET:].astype(jnp.float32).reshape(8, 2, PEAK_ROWS // 2, HEAD)
    peaks = jnp.max(peaks, axis=(0, 2, 3))[::-1]
    for axis in ("y", "z"):
        with jax.named_scope("peaks"):
            peaks = jnp.max(spread(peaks, axis).reshape(-1, 2), axis=0)
    return attended, peaks / FP_TOP


def solution(mesh):
    fine = Mesh(mesh.devices.reshape(4, 4, 16, 2), AXES)
    rows, columns = ("z", "core"), ("y", "x")
    return jax.shard_map(
        local,
        mesh=fine,
        in_specs=(P(rows, columns, None, None), P(None, AXES), P(), P(rows, None)),
        out_specs=(P(rows, columns, None, None), P()),
        check_vma=False,
    )
```

```python
import math

import jax
import jax.numpy as jnp
from jax import lax
from jax.experimental import pallas as pl
from jax.experimental.pallas import tpu as pltpu
from jax.sharding import Mesh
from jax.sharding import PartitionSpec as P

HEADS = 8
HEAD = 128
D = 2048
COLS = 64
ROWS = 4
HALO = 3
BLOCK = 16
SET = ROWS * COLS
KV_ROWS = (BLOCK + 2 * HALO) * COLS
FP_TOP = 448.0
AXES = ("y", "x", "z", "core")
GROUP = ("x", "core")
PEAK_ROWS = 16
NEG = -1e30


def device_of(y, x, z, core):
    return ((y * 4 + x) * 16 + z) * 2 + core


def head_permutations():
    main, extra = [], []
    for tile in range(16):
        m, odd = divmod(tile, 2)
        for shard in range(32):
            z, core = divmod(shard, 2)
            source = tile * 32 + shard
            cut = 10 if odd else 21
            first = 3 * m + odd

            def target(block):
                head = block % HEADS
                return device_of(2 * odd + core, head // 2, z, head % 2)

            main.append((source, target(first if shard <= cut else first + 1)))
            if shard == cut:
                extra.append((source, target(first + 1)))
    return main, extra


def column_order(head):
    d = lax.broadcasted_iota(jnp.int32, (3 * HEAD, 3 * HEAD), 1)
    r = lax.broadcasted_iota(jnp.int32, (3 * HEAD, 3 * HEAD), 0)
    natural = ((head + 2 * (d // HEAD)) % 3) * HEAD + d % HEAD
    half, m = natural // 192, natural % 192
    z, core, j = m // 12, (m % 12) // 6, m % 6
    return ((2 * half + core) * 96 + z * 6 + j == r).astype(jnp.bfloat16)


def project_kernel(scale_ref, x_ref, w_ref, order_ref, qkv_ref, top_ref, bottom_ref, w_scr):
    scale = scale_ref[0]
    inverse = 1.0 / scale
    w_scr[...] = lax.dot_general(
        order_ref[...], w_ref[...], (((0,), (0,)), ((), ())), preferred_element_type=jnp.float32
    ).astype(jnp.bfloat16)
    for part in range(4):
        tokens = x_ref[2 * part : 2 * part + 2].reshape(2 * SET, D)
        tokens = (tokens.astype(jnp.float32) * inverse).astype(jnp.bfloat16)
        tokens = jnp.clip(tokens, -FP_TOP, FP_TOP)
        out = lax.dot_general(
            tokens, w_scr[...], (((1,), (1,)), ((), ())), preferred_element_type=jnp.float32
        )
        out = (out * scale).astype(jnp.bfloat16).reshape(2, SET, 3 * HEAD)
        qkv_ref[2 * part : 2 * part + 2] = out
        if part == 0:
            top_ref[...] = out[:, : HALO * COLS, HEAD:]
        if part == 3:
            bottom_ref[...] = out[:, SET - HALO * COLS :, HEAD:]


def project(scale, tokens, weights, order):
    halo = jax.ShapeDtypeStruct((2, HALO * COLS, 2 * HEAD), jnp.bfloat16)
    vmem = pl.BlockSpec(memory_space=pltpu.VMEM)
    return pl.pallas_call(
        project_kernel,
        out_shape=(jax.ShapeDtypeStruct((8, SET, 3 * HEAD), jnp.bfloat16), halo, halo),
        in_specs=[pl.BlockSpec(memory_space=pltpu.SMEM), vmem, vmem, vmem],
        out_specs=(vmem, vmem, vmem),
        scratch_shapes=[pltpu.VMEM((3 * HEAD, D), jnp.bfloat16)],
        compiler_params=pltpu.CompilerParams(vmem_limit_bytes=24 * 2**20),
        cost_estimate=pl.CostEstimate(
            flops=2 * 8 * SET * D * 3 * HEAD, bytes_accessed=12 * 2**20, transcendentals=0
        ),
        name="project",
    )(scale, tokens, weights, order)


def attend_kernel(place_ref, peak_ref, qkv_ref, above_ref, below_ref, out_ref, kv):
    base = place_ref[0]
    scaling = float(HEAD) ** -0.5
    shape = (2 * COLS, 8 * COLS)
    q_row = lax.broadcasted_iota(jnp.int32, shape, 0)
    k_row = lax.broadcasted_iota(jnp.int32, shape, 1)
    row_step = k_row // COLS - q_row // COLS
    col_step = k_row % COLS - q_row % COLS
    window = (row_step >= 0) & (row_step <= 2 * HALO) & (col_step >= -HALO) & (col_step <= HALO)
    window = jnp.where(window, 0.0, NEG)
    centre = jnp.where((row_step == HALO) & (col_step == 0), 0.0, NEG)
    key_at = lax.broadcasted_iota(jnp.int32, (1, 8 * COLS), 1)
    query_at = lax.broadcasted_iota(jnp.int32, (2 * COLS, 1), 0)
    highest = jnp.zeros((2 * COLS, HEAD), jnp.float32)
    for image in range(2):
        ext_rows, ext_cols = place_ref[1 + 2 * image], place_ref[2 + 2 * image]
        kv[image, : HALO * COLS] = above_ref[image]
        for part in range(4):
            start = HALO * COLS + part * SET
            kv[image, start : start + SET] = qkv_ref[2 * part + image, :, HEAD:]
        kv[image, KV_ROWS - HALO * COLS :] = below_ref[image]
        for pair in range(BLOCK // 2):
            part, inner = pair // 2, (pair % 2) * 2 * COLS
            query = qkv_ref[2 * part + image, inner : inner + 2 * COLS, :HEAD]
            start = 2 * pair * COLS
            keys = kv[image, start : start + 8 * COLS, :HEAD]
            values = kv[image, start : start + 8 * COLS, HEAD:]
            scores = lax.dot_general(
                query, keys, (((1,), (1,)), ((), ())), preferred_element_type=jnp.float32
            )
            key_rows = base + (2 * pair - HALO) + key_at // COLS
            key_cols = key_at % COLS
            valid = (key_rows >= 0) & (key_rows < ext_rows) & (key_cols < ext_cols)
            bias = jnp.where(valid, window, centre)
            scores = scores * scaling + bias
            weights = jnp.exp(scores - jnp.max(scores, axis=1, keepdims=True))
            weights = weights * (1.0 / jnp.sum(weights, axis=1, keepdims=True))
            result = jnp.dot(
                weights.astype(jnp.bfloat16), values, preferred_element_type=jnp.float32
            )
            inside = (base + 2 * pair + query_at // COLS < ext_rows) & (query_at % COLS < ext_cols)
            result = jnp.where(inside, result, 0.0).astype(jnp.bfloat16)
            highest = jnp.maximum(highest, jnp.abs(result.astype(jnp.float32)))
            out_ref[2 * part + image, inner : inner + 2 * COLS, :] = result
    lines = lax.broadcasted_iota(jnp.int32, (PEAK_ROWS, HEAD), 0)
    peaks = jnp.where(lines < PEAK_ROWS // 2, peak_ref[0], jnp.max(highest)).astype(jnp.bfloat16)
    for group in range(8):
        out_ref[group, SET:, :] = peaks


def attend(place, peak_in, qkv, above, below):
    vmem = pl.BlockSpec(memory_space=pltpu.VMEM)
    smem = pl.BlockSpec(memory_space=pltpu.SMEM)
    return pl.pallas_call(
        attend_kernel,
        out_shape=jax.ShapeDtypeStruct((8, SET + PEAK_ROWS, HEAD), jnp.bfloat16),
        in_specs=[smem, smem, vmem, vmem, vmem],
        out_specs=vmem,
        scratch_shapes=[pltpu.VMEM((2, KV_ROWS, 2 * HEAD), jnp.bfloat16)],
        compiler_params=pltpu.CompilerParams(vmem_limit_bytes=24 * 2**20),
        cost_estimate=pl.CostEstimate(
            flops=4 * 16 * 128 * 512 * HEAD, bytes_accessed=3 * 2**20, transcendentals=16 * 128 * 512
        ),
        name="attend",
    )(place, peak_in, qkv, above, below)


def spread(value, axis):
    size = math.prod(lax.axis_size(name) for name in ((axis,) if isinstance(axis, str) else axis))
    copies = jnp.broadcast_to(value[None], (size,) + value.shape)
    return lax.all_to_all(copies, axis, 0, 0, tiled=True)


def shift(value, axis, step):
    size = lax.axis_size(axis)
    return lax.ppermute(value, axis, [(i, (i + step) % size) for i in range(size)])


def head_weights(w_qkv, images):
    main, extra = head_permutations()
    mine = w_qkv.T
    first = lax.ppermute(mine, AXES, main)
    second = lax.ppermute(mine, AXES, extra)
    y, z = lax.axis_index("y"), lax.axis_index("z")
    shard = 2 * z + y % 2
    cut = jnp.where((y < 2) & (shard == 21), 2, jnp.where((y >= 2) & (shard == 10), 4, 6))
    column = lax.broadcasted_iota(jnp.int32, mine.shape, 0)
    merged = jnp.where(column < cut, first, second)
    with jax.named_scope("weights_over_z"):
        over_z = spread(merged.reshape(96, 128), "z").reshape(96, D)
    over_z, late = lax.optimization_barrier((over_z, images))
    with jax.named_scope("weights_over_y"):
        return spread(over_z, "y").reshape(3 * HEAD, D), late


def local(images, w_qkv, prev_scale, extent):
    with jax.named_scope("tokens"):
        tokens = lax.all_gather(images.reshape(SET, D), GROUP, axis=0, tiled=False)
    weights, late = head_weights(w_qkv, images)
    peak_in = jnp.max(jnp.abs(late)).astype(jnp.float32).reshape(1)
    core = lax.axis_index("core")
    order = column_order(2 * lax.axis_index("x") + core)
    other = shift(extent, "core", 1)
    extents = jnp.where(core == 0, jnp.concatenate([extent, other]), jnp.concatenate([other, extent]))
    place = jnp.stack([lax.axis_index("y") * BLOCK, *extents.reshape(4)]).astype(jnp.int32)
    qkv, top, bottom = project(prev_scale, tokens, weights, order)
    with jax.named_scope("halo"):
        above = lax.ppermute(bottom, "y", [(i, i + 1) for i in range(3)])
        below = lax.ppermute(top, "y", [(i + 1, i) for i in range(3)])
    mixed = attend(place, peak_in, qkv, above, below)
    with jax.named_scope("heads"):
        mixed = lax.all_to_all(mixed, GROUP, 0, 0, tiled=True)
    attended = mixed[:, :SET].transpose(1, 0, 2).reshape(1, ROWS, COLS, HEADS * HEAD)
    peaks = mixed[:, SET:].astype(jnp.float32).reshape(8, 2, PEAK_ROWS // 2, HEAD)
    peaks = jnp.max(peaks, axis=(0, 2, 3))
    for axis in ("y", "z"):
        with jax.named_scope("peaks"):
            peaks = jnp.max(spread(peaks, axis).reshape(-1, 2), axis=0)
    return attended, peaks / FP_TOP


def solution(mesh):
    fine = Mesh(mesh.devices.reshape(4, 4, 16, 2), AXES)
    rows, columns = ("z", "core"), ("y", "x")
    return jax.shard_map(
        local,
        mesh=fine,
        in_specs=(P(rows, columns, None, None), P(None, AXES), P(), P(rows, None)),
        out_specs=(P(rows, columns, None, None), P()),
        check_vma=False,
    )
```

```python
import math

import jax
import jax.numpy as jnp
from jax import lax
from jax.experimental import pallas as pl
from jax.experimental.pallas import tpu as pltpu
from jax.sharding import Mesh
from jax.sharding import PartitionSpec as P

HEADS = 8
HEAD = 128
D = 2048
COLS = 64
ROWS = 4
HALO = 3
BLOCK = 16
SET = ROWS * COLS
KV_ROWS = (BLOCK + 2 * HALO) * COLS
FP_TOP = 448.0
AXES = ("y", "x", "z", "core")
GROUP = ("x", "core")
PEAK_ROWS = 16
INNER = (2, 3, 4, 5)
NEG = -1e30


def device_of(y, x, z, core):
    return ((y * 4 + x) * 16 + z) * 2 + core


def head_permutations():
    main, extra = [], []
    for tile in range(16):
        m, odd = divmod(tile, 2)
        for shard in range(32):
            z, core = divmod(shard, 2)
            source = tile * 32 + shard
            cut = 10 if odd else 21
            first = 3 * m + odd

            def target(block):
                head = block % HEADS
                return device_of(2 * odd + core, head // 2, z, head % 2)

            main.append((source, target(first if shard <= cut else first + 1)))
            if shard == cut:
                extra.append((source, target(first + 1)))
    return main, extra


def column_order(head, y):
    d = lax.broadcasted_iota(jnp.int32, (3 * HEAD, 3 * HEAD), 1)
    r = lax.broadcasted_iota(jnp.int32, (3 * HEAD, 3 * HEAD), 0)
    natural = ((head + 2 * (d // HEAD)) % 3) * HEAD + d % HEAD
    half, m = natural // 192, natural % 192
    z, core, j = m // 12, (m % 12) // 6, m % 6
    away = (2 * half + core + 4 - y) % 4
    place = jnp.where(away == 3, 1, jnp.where(away == 0, 0, away + 1))
    return (place * 96 + z * 6 + j == r).astype(jnp.bfloat16)


def project_kernel(scale_ref, x_ref, w0_ref, w1_ref, w2_ref, w3_ref, order_ref, qkv_ref, top_ref, bottom_ref, w_cat, w_scr):
    scale = scale_ref[0]
    inverse = 1.0 / scale
    for part, ref in enumerate((w0_ref, w1_ref, w2_ref, w3_ref)):
        w_cat[96 * part : 96 * (part + 1)] = ref[...]
    w_scr[...] = lax.dot_general(
        order_ref[...], w_cat[...], (((0,), (0,)), ((), ())), preferred_element_type=jnp.float32
    ).astype(jnp.bfloat16)
    for part in range(4):
        tokens = x_ref[2 * part : 2 * part + 2].reshape(2 * SET, D)
        tokens = (tokens.astype(jnp.float32) * inverse).astype(jnp.bfloat16)
        tokens = jnp.clip(tokens, -FP_TOP, FP_TOP)
        out = lax.dot_general(
            tokens, w_scr[...], (((1,), (1,)), ((), ())), preferred_element_type=jnp.float32
        )
        out = (out * scale).astype(jnp.bfloat16).reshape(2, SET, 3 * HEAD)
        qkv_ref[2 * part : 2 * part + 2] = out
        if part == 0:
            top_ref[...] = out[:, : HALO * COLS, HEAD:]
        if part == 3:
            bottom_ref[...] = out[:, SET - HALO * COLS :, HEAD:]


def project(scale, tokens, weights, order):
    halo = jax.ShapeDtypeStruct((2, HALO * COLS, 2 * HEAD), jnp.bfloat16)
    vmem = pl.BlockSpec(memory_space=pltpu.VMEM)
    return pl.pallas_call(
        project_kernel,
        out_shape=(jax.ShapeDtypeStruct((8, SET, 3 * HEAD), jnp.bfloat16), halo, halo),
        in_specs=[pl.BlockSpec(memory_space=pltpu.SMEM)] + [vmem] * 6,
        out_specs=(vmem, vmem, vmem),
        scratch_shapes=[pltpu.VMEM((3 * HEAD, D), jnp.bfloat16)] * 2,
        compiler_params=pltpu.CompilerParams(vmem_limit_bytes=24 * 2**20),
        cost_estimate=pl.CostEstimate(
            flops=2 * 8 * SET * D * 3 * HEAD, bytes_accessed=12 * 2**20, transcendentals=0
        ),
        name="project",
    )(scale, tokens, *weights, order)


def attend_rows(pairs, place_ref, qkv_ref, out_ref, kv):
    base = place_ref[0]
    scaling = float(HEAD) ** -0.5
    shape = (2 * COLS, 8 * COLS)
    q_row = lax.broadcasted_iota(jnp.int32, shape, 0)
    k_row = lax.broadcasted_iota(jnp.int32, shape, 1)
    row_step = k_row // COLS - q_row // COLS
    col_step = k_row % COLS - q_row % COLS
    window = (row_step >= 0) & (row_step <= 2 * HALO) & (col_step >= -HALO) & (col_step <= HALO)
    window = jnp.where(window, 0.0, NEG)
    centre = jnp.where((row_step == HALO) & (col_step == 0), 0.0, NEG)
    key_at = lax.broadcasted_iota(jnp.int32, (1, 8 * COLS), 1)
    query_at = lax.broadcasted_iota(jnp.int32, (2 * COLS, 1), 0)
    highest = jnp.zeros((2 * COLS, HEAD), jnp.float32)
    for image in range(2):
        ext_rows, ext_cols = place_ref[1 + 2 * image], place_ref[2 + 2 * image]
        for pair in pairs:
            part, inner = pair // 2, (pair % 2) * 2 * COLS
            query = qkv_ref[2 * part + image, inner : inner + 2 * COLS, :HEAD]
            start = 2 * pair * COLS
            keys = kv[image, start : start + 8 * COLS, :HEAD]
            values = kv[image, start : start + 8 * COLS, HEAD:]
            scores = lax.dot_general(
                query, keys, (((1,), (1,)), ((), ())), preferred_element_type=jnp.float32
            )
            key_rows = base + (2 * pair - HALO) + key_at // COLS
            key_cols = key_at % COLS
            valid = (key_rows >= 0) & (key_rows < ext_rows) & (key_cols < ext_cols)
            bias = jnp.where(valid, window, centre)
            scores = scores * scaling + bias
            weights = jnp.exp(scores - jnp.max(scores, axis=1, keepdims=True))
            weights = weights * (1.0 / jnp.sum(weights, axis=1, keepdims=True))
            result = jnp.dot(
                weights.astype(jnp.bfloat16), values, preferred_element_type=jnp.float32
            )
            inside = (base + 2 * pair + query_at // COLS < ext_rows) & (query_at % COLS < ext_cols)
            result = jnp.where(inside, result, 0.0).astype(jnp.bfloat16)
            highest = jnp.maximum(highest, jnp.abs(result.astype(jnp.float32)))
            out_ref[2 * part + image, inner : inner + 2 * COLS, :] = result
    return highest


def fill_keys(qkv_ref, kv):
    for image in range(2):
        for part in range(4):
            start = HALO * COLS + part * SET
            kv[image, start : start + SET] = qkv_ref[2 * part + image, :, HEAD:]


def attend_inner_kernel(place_ref, qkv_ref, out_ref, highest_ref, kv):
    fill_keys(qkv_ref, kv)
    highest_ref[...] = attend_rows(INNER, place_ref, qkv_ref, out_ref, kv)


def attend_outer_kernel(place_ref, peak_ref, qkv_ref, above_ref, below_ref, inner_ref, highest_ref, out_ref, kv):
    for image in range(2):
        kv[image, : HALO * COLS] = above_ref[image]
        kv[image, KV_ROWS - HALO * COLS :] = below_ref[image]
    fill_keys(qkv_ref, kv)
    for image in range(2):
        for pair in INNER:
            place = 2 * (pair // 2) + image, slice((pair % 2) * 2 * COLS, (pair % 2 + 1) * 2 * COLS)
            out_ref[place] = inner_ref[place]
    outer = [pair for pair in range(BLOCK // 2) if pair not in INNER]
    highest = jnp.maximum(attend_rows(outer, place_ref, qkv_ref, out_ref, kv), highest_ref[...])
    lines = lax.broadcasted_iota(jnp.int32, (PEAK_ROWS, HEAD), 0)
    peaks = jnp.where(lines < PEAK_ROWS // 2, peak_ref[0], jnp.max(highest)).astype(jnp.bfloat16)
    for group in range(8):
        out_ref[group, SET:, :] = peaks


def attend_inner(place, qkv):
    vmem = pl.BlockSpec(memory_space=pltpu.VMEM)
    return pl.pallas_call(
        attend_inner_kernel,
        out_shape=(
            jax.ShapeDtypeStruct((8, SET, HEAD), jnp.bfloat16),
            jax.ShapeDtypeStruct((2 * COLS, HEAD), jnp.float32),
        ),
        in_specs=[pl.BlockSpec(memory_space=pltpu.SMEM), vmem],
        out_specs=(vmem, vmem),
        scratch_shapes=[pltpu.VMEM((2, KV_ROWS, 2 * HEAD), jnp.bfloat16)],
        compiler_params=pltpu.CompilerParams(vmem_limit_bytes=24 * 2**20),
        cost_estimate=pl.CostEstimate(
            flops=4 * 8 * 128 * 512 * HEAD, bytes_accessed=2 * 2**20, transcendentals=8 * 128 * 512
        ),
        name="attend_inner",
    )(place, qkv)


def attend_outer(place, peak_in, qkv, above, below, inner, highest):
    vmem = pl.BlockSpec(memory_space=pltpu.VMEM)
    smem = pl.BlockSpec(memory_space=pltpu.SMEM)
    return pl.pallas_call(
        attend_outer_kernel,
        out_shape=jax.ShapeDtypeStruct((8, SET + PEAK_ROWS, HEAD), jnp.bfloat16),
        in_specs=[smem, smem] + [vmem] * 5,
        out_specs=vmem,
        scratch_shapes=[pltpu.VMEM((2, KV_ROWS, 2 * HEAD), jnp.bfloat16)],
        compiler_params=pltpu.CompilerParams(vmem_limit_bytes=24 * 2**20),
        cost_estimate=pl.CostEstimate(
            flops=4 * 8 * 128 * 512 * HEAD, bytes_accessed=3 * 2**20, transcendentals=8 * 128 * 512
        ),
        name="attend_outer",
    )(place, peak_in, qkv, above, below, inner, highest)


def spread(value, axis):
    size = math.prod(lax.axis_size(name) for name in ((axis,) if isinstance(axis, str) else axis))
    copies = jnp.broadcast_to(value[None], (size,) + value.shape)
    return lax.all_to_all(copies, axis, 0, 0, tiled=True)


def shift(value, axis, step):
    size = lax.axis_size(axis)
    return lax.ppermute(value, axis, [(i, (i + step) % size) for i in range(size)])


def head_weights(w_qkv, images):
    main, extra = head_permutations()
    mine = w_qkv.T
    first = lax.ppermute(mine, AXES, main)
    second = lax.ppermute(mine, AXES, extra)
    y, z = lax.axis_index("y"), lax.axis_index("z")
    shard = 2 * z + y % 2
    cut = jnp.where((y < 2) & (shard == 21), 2, jnp.where((y >= 2) & (shard == 10), 4, 6))
    column = lax.broadcasted_iota(jnp.int32, mine.shape, 0)
    merged = jnp.where(column < cut, first, second)
    with jax.named_scope("weights_over_z"):
        over_z = spread(merged.reshape(96, 128), "z").reshape(96, D)
    over_z, late = lax.optimization_barrier((over_z, images))
    with jax.named_scope("weights_over_y"):
        return [over_z] + [shift(over_z, "y", step) for step in (1, -1, 2)], late


def local(images, w_qkv, prev_scale, extent):
    with jax.named_scope("tokens"):
        tokens = lax.all_gather(images.reshape(SET, D), GROUP, axis=0, tiled=False)
    weights, late = head_weights(w_qkv, images)
    peak_in = jnp.max(jnp.abs(late)).astype(jnp.float32).reshape(1)
    core = lax.axis_index("core")
    order = column_order(2 * lax.axis_index("x") + core, lax.axis_index("y"))
    other = shift(extent, "core", 1)
    extents = jnp.where(core == 0, jnp.concatenate([extent, other]), jnp.concatenate([other, extent]))
    place = jnp.stack([lax.axis_index("y") * BLOCK, *extents.reshape(4)]).astype(jnp.int32)
    qkv, top, bottom = project(prev_scale, tokens, weights, order)
    with jax.named_scope("halo"):
        above = lax.ppermute(bottom, "y", [(i, i + 1) for i in range(3)])
        below = lax.ppermute(top, "y", [(i + 1, i) for i in range(3)])
    inner, highest = attend_inner(place, qkv)
    mixed = attend_outer(place, peak_in, qkv, above, below, inner, highest)
    with jax.named_scope("heads"):
        mixed = lax.all_to_all(mixed, GROUP, 0, 0, tiled=True)
    attended = mixed[:, :SET].transpose(1, 0, 2).reshape(1, ROWS, COLS, HEADS * HEAD)
    peaks = mixed[:, SET:].astype(jnp.float32).reshape(8, 2, PEAK_ROWS // 2, HEAD)
    peaks = jnp.max(peaks, axis=(0, 2, 3))
    for axis in ("y", "z"):
        with jax.named_scope("peaks"):
            peaks = jnp.max(spread(peaks, axis).reshape(-1, 2), axis=0)
    return attended, peaks / FP_TOP


def solution(mesh):
    fine = Mesh(mesh.devices.reshape(4, 4, 16, 2), AXES)
    rows, columns = ("z", "core"), ("y", "x")
    return jax.shard_map(
        local,
        mesh=fine,
        in_specs=(P(rows, columns, None, None), P(None, AXES), P(), P(rows, None)),
        out_specs=(P(rows, columns, None, None), P()),
        check_vma=False,
    )
```

```python
import math

import jax
import jax.numpy as jnp
from jax import lax
from jax.experimental import pallas as pl
from jax.experimental.pallas import tpu as pltpu
from jax.sharding import Mesh
from jax.sharding import PartitionSpec as P

HEADS = 8
HEAD = 128
D = 2048
COLS = 64
ROWS = 4
HALO = 3
BLOCK = 16
SET = ROWS * COLS
KV_ROWS = (BLOCK + 2 * HALO) * COLS
FP_TOP = 448.0
AXES = ("y", "x", "z", "core")
GROUP = ("x", "core")
PEAK_ROWS = 16
KEYS = (ROWS + 2 * HALO) * COLS
NEG = -1e30


def device_of(y, x, z, core):
    return ((y * 4 + x) * 16 + z) * 2 + core


def head_permutations():
    main, extra = [], []
    for tile in range(16):
        m, odd = divmod(tile, 2)
        for shard in range(32):
            z, core = divmod(shard, 2)
            source = tile * 32 + shard
            cut = 10 if odd else 21
            first = 3 * m + odd

            def target(block):
                head = block % HEADS
                return device_of(2 * odd + core, head // 2, z, head % 2)

            main.append((source, target(first if shard <= cut else first + 1)))
            if shard == cut:
                extra.append((source, target(first + 1)))
    return main, extra


def column_order(head, y):
    d = lax.broadcasted_iota(jnp.int32, (3 * HEAD, 3 * HEAD), 1)
    r = lax.broadcasted_iota(jnp.int32, (3 * HEAD, 3 * HEAD), 0)
    natural = ((head + 2 * (d // HEAD)) % 3) * HEAD + d % HEAD
    half, m = natural // 192, natural % 192
    z, core, j = m // 12, (m % 12) // 6, m % 6
    away = (2 * half + core + 4 - y) % 4
    place = jnp.where(away == 3, 1, jnp.where(away == 0, 0, away + 1))
    return (place * 96 + z * 6 + j == r).astype(jnp.bfloat16)


def project_kernel(scale_ref, x_ref, w0_ref, w1_ref, w2_ref, w3_ref, order_ref, qkv_ref, top_ref, bottom_ref, w_cat, w_scr):
    scale = scale_ref[0]
    inverse = 1.0 / scale
    for part, ref in enumerate((w0_ref, w1_ref, w2_ref, w3_ref)):
        w_cat[96 * part : 96 * (part + 1)] = ref[...]
    w_scr[...] = lax.dot_general(
        order_ref[...], w_cat[...], (((0,), (0,)), ((), ())), preferred_element_type=jnp.float32
    ).astype(jnp.bfloat16)
    for part in range(4):
        tokens = x_ref[2 * part : 2 * part + 2].reshape(2 * SET, D)
        tokens = (tokens.astype(jnp.float32) * inverse).astype(jnp.bfloat16)
        tokens = jnp.clip(tokens, -FP_TOP, FP_TOP)
        out = lax.dot_general(
            tokens, w_scr[...], (((1,), (1,)), ((), ())), preferred_element_type=jnp.float32
        )
        out = (out * scale).astype(jnp.bfloat16).reshape(2, SET, 3 * HEAD)
        qkv_ref[2 * part : 2 * part + 2] = out
        if part == 0:
            top_ref[...] = out[:, : HALO * COLS, HEAD:]
        if part == 3:
            bottom_ref[...] = out[:, SET - HALO * COLS :, HEAD:]


def project(scale, tokens, weights, order):
    halo = jax.ShapeDtypeStruct((2, HALO * COLS, 2 * HEAD), jnp.bfloat16)
    vmem = pl.BlockSpec(memory_space=pltpu.VMEM)
    return pl.pallas_call(
        project_kernel,
        out_shape=(jax.ShapeDtypeStruct((8, SET, 3 * HEAD), jnp.bfloat16), halo, halo),
        in_specs=[pl.BlockSpec(memory_space=pltpu.SMEM)] + [vmem] * 6,
        out_specs=(vmem, vmem, vmem),
        scratch_shapes=[pltpu.VMEM((3 * HEAD, D), jnp.bfloat16)] * 2,
        compiler_params=pltpu.CompilerParams(vmem_limit_bytes=24 * 2**20),
        cost_estimate=pl.CostEstimate(
            flops=2 * 8 * SET * D * 3 * HEAD, bytes_accessed=12 * 2**20, transcendentals=0
        ),
        name="project",
    )(scale, tokens, *weights, order)


def attend_rows(units, place_ref, qkv_ref, out_ref, kv):
    base = place_ref[0]
    scaling = float(HEAD) ** -0.5 * math.log2(math.e)
    shape = (SET, KEYS)
    q_row = lax.broadcasted_iota(jnp.int32, shape, 0)
    k_row = lax.broadcasted_iota(jnp.int32, shape, 1)
    row_step = k_row // COLS - q_row // COLS
    col_step = k_row % COLS - q_row % COLS
    window = (row_step >= 0) & (row_step <= 2 * HALO) & (col_step >= -HALO) & (col_step <= HALO)
    window = jnp.where(window, 0.0, NEG)
    centre = jnp.where((row_step == HALO) & (col_step == 0), 0.0, NEG)
    key_at = lax.broadcasted_iota(jnp.int32, (1, KEYS), 1)
    query_at = lax.broadcasted_iota(jnp.int32, (SET, 1), 0)
    highest = jnp.zeros((SET, HEAD), jnp.float32)
    for image in range(2):
        ext_rows, ext_cols = place_ref[1 + 2 * image], place_ref[2 + 2 * image]
        for unit in units:
            query = qkv_ref[2 * unit + image, :, :HEAD]
            start = unit * SET
            keys = kv[image, start : start + KEYS, :HEAD]
            values = kv[image, start : start + KEYS, HEAD:]
            scores = lax.dot_general(
                query, keys, (((1,), (1,)), ((), ())), preferred_element_type=jnp.float32
            )
            key_rows = base + (ROWS * unit - HALO) + key_at // COLS
            key_cols = key_at % COLS
            valid = (key_rows >= 0) & (key_rows < ext_rows) & (key_cols < ext_cols)
            bias = jnp.where(valid, window, centre)
            scores = scores * scaling + bias
            weights = jnp.exp2(scores - jnp.max(scores, axis=1, keepdims=True))
            weights = weights * (1.0 / jnp.sum(weights, axis=1, keepdims=True))
            result = jnp.dot(
                weights.astype(jnp.bfloat16), values, preferred_element_type=jnp.float32
            )
            inside = (base + ROWS * unit + query_at // COLS < ext_rows) & (query_at % COLS < ext_cols)
            result = jnp.where(inside, result, 0.0).astype(jnp.bfloat16)
            highest = jnp.maximum(highest, jnp.abs(result.astype(jnp.float32)))
            out_ref[2 * unit + image, :SET] = result
    return highest


def fill_keys(qkv_ref, kv):
    for image in range(2):
        for part in range(4):
            start = HALO * COLS + part * SET
            kv[image, start : start + SET] = qkv_ref[2 * part + image, :, HEAD:]


def attend_inner_kernel(place_ref, qkv_ref, out_ref, highest_ref, kv):
    fill_keys(qkv_ref, kv)
    highest_ref[...] = attend_rows((1, 2), place_ref, qkv_ref, out_ref, kv)


def attend_outer_kernel(place_ref, peak_ref, qkv_ref, above_ref, below_ref, inner_ref, highest_ref, out_ref, kv):
    for image in range(2):
        kv[image, : HALO * COLS] = above_ref[image]
        kv[image, KV_ROWS - HALO * COLS :] = below_ref[image]
    fill_keys(qkv_ref, kv)
    for group in range(2, 6):
        out_ref[group, :SET] = inner_ref[group]
    highest = jnp.maximum(attend_rows((0, 3), place_ref, qkv_ref, out_ref, kv), highest_ref[...])
    lines = lax.broadcasted_iota(jnp.int32, (PEAK_ROWS, HEAD), 0)
    peaks = jnp.where(lines < PEAK_ROWS // 2, peak_ref[0], jnp.max(highest)).astype(jnp.bfloat16)
    for group in range(8):
        out_ref[group, SET:, :] = peaks


def attend_inner(place, qkv):
    vmem = pl.BlockSpec(memory_space=pltpu.VMEM)
    return pl.pallas_call(
        attend_inner_kernel,
        out_shape=(
            jax.ShapeDtypeStruct((8, SET, HEAD), jnp.bfloat16),
            jax.ShapeDtypeStruct((SET, HEAD), jnp.float32),
        ),
        in_specs=[pl.BlockSpec(memory_space=pltpu.SMEM), vmem],
        out_specs=(vmem, vmem),
        scratch_shapes=[pltpu.VMEM((2, KV_ROWS, 2 * HEAD), jnp.bfloat16)],
        compiler_params=pltpu.CompilerParams(vmem_limit_bytes=24 * 2**20),
        cost_estimate=pl.CostEstimate(
            flops=4 * 4 * SET * KEYS * HEAD, bytes_accessed=2 * 2**20, transcendentals=4 * SET * KEYS
        ),
        name="attend_inner",
    )(place, qkv)


def attend_outer(place, peak_in, qkv, above, below, inner, highest):
    vmem = pl.BlockSpec(memory_space=pltpu.VMEM)
    smem = pl.BlockSpec(memory_space=pltpu.SMEM)
    return pl.pallas_call(
        attend_outer_kernel,
        out_shape=jax.ShapeDtypeStruct((8, SET + PEAK_ROWS, HEAD), jnp.bfloat16),
        in_specs=[smem, smem] + [vmem] * 5,
        out_specs=vmem,
        scratch_shapes=[pltpu.VMEM((2, KV_ROWS, 2 * HEAD), jnp.bfloat16)],
        compiler_params=pltpu.CompilerParams(vmem_limit_bytes=24 * 2**20),
        cost_estimate=pl.CostEstimate(
            flops=4 * 4 * SET * KEYS * HEAD, bytes_accessed=3 * 2**20, transcendentals=4 * SET * KEYS
        ),
        name="attend_outer",
    )(place, peak_in, qkv, above, below, inner, highest)


def spread(value, axis):
    size = math.prod(lax.axis_size(name) for name in ((axis,) if isinstance(axis, str) else axis))
    copies = jnp.broadcast_to(value[None], (size,) + value.shape)
    return lax.all_to_all(copies, axis, 0, 0, tiled=True)


def shift(value, axis, step):
    size = lax.axis_size(axis)
    return lax.ppermute(value, axis, [(i, (i + step) % size) for i in range(size)])


def head_weights(w_qkv, images):
    main, extra = head_permutations()
    mine = w_qkv.T
    first = lax.ppermute(mine, AXES, main)
    second = lax.ppermute(mine, AXES, extra)
    y, z = lax.axis_index("y"), lax.axis_index("z")
    shard = 2 * z + y % 2
    cut = jnp.where((y < 2) & (shard == 21), 2, jnp.where((y >= 2) & (shard == 10), 4, 6))
    column = lax.broadcasted_iota(jnp.int32, mine.shape, 0)
    merged = jnp.where(column < cut, first, second)
    with jax.named_scope("weights_over_z"):
        over_z = spread(merged.reshape(96, 128), "z").reshape(96, D)
    over_z, late = lax.optimization_barrier((over_z, images))
    with jax.named_scope("weights_over_y"):
        return [over_z] + [shift(over_z, "y", step) for step in (1, -1, 2)], late


def local(images, w_qkv, prev_scale, extent):
    with jax.named_scope("tokens"):
        tokens = lax.all_gather(images.reshape(SET, D), GROUP, axis=0, tiled=False)
    weights, late = head_weights(w_qkv, images)
    core = lax.axis_index("core")
    order = column_order(2 * lax.axis_index("x") + core, lax.axis_index("y"))
    other = shift(extent, "core", 1)
    peak_in = jnp.max(jnp.abs(late)).astype(jnp.float32).reshape(1)
    extents = jnp.where(core == 0, jnp.concatenate([extent, other]), jnp.concatenate([other, extent]))
    place = jnp.stack([lax.axis_index("y") * BLOCK, *extents.reshape(4)]).astype(jnp.int32)
    order, peak_in, place = lax.optimization_barrier((order, peak_in, place))
    qkv, top, bottom = project(prev_scale, tokens, weights, order)
    with jax.named_scope("halo"):
        above = lax.ppermute(bottom, "y", [(i, i + 1) for i in range(3)])
        below = lax.ppermute(top, "y", [(i + 1, i) for i in range(3)])
    inner, highest = attend_inner(place, qkv)
    mixed = attend_outer(place, peak_in, qkv, above, below, inner, highest)
    with jax.named_scope("heads"):
        mixed = lax.all_to_all(mixed, GROUP, 0, 0, tiled=True)
    attended = mixed[:, :SET].transpose(1, 0, 2).reshape(1, ROWS, COLS, HEADS * HEAD)
    peaks = mixed[:, SET:].astype(jnp.float32).reshape(8, 2, PEAK_ROWS // 2, HEAD)
    peaks = jnp.max(peaks, axis=(0, 2, 3))
    for axis in ("y", "z"):
        with jax.named_scope("peaks"):
            peaks = jnp.max(spread(peaks, axis).reshape(-1, 2), axis=0)
    return attended, peaks / FP_TOP


def solution(mesh):
    fine = Mesh(mesh.devices.reshape(4, 4, 16, 2), AXES)
    rows, columns = ("z", "core"), ("y", "x")
    return jax.shard_map(
        local,
        mesh=fine,
        in_specs=(P(rows, columns, None, None), P(None, AXES), P(), P(rows, None)),
        out_specs=(P(rows, columns, None, None), P()),
        check_vma=False,
    )
```

```python
import math

import jax
import jax.numpy as jnp
from jax import lax
from jax.experimental import pallas as pl
from jax.experimental.pallas import tpu as pltpu
from jax.sharding import Mesh
from jax.sharding import PartitionSpec as P

HEADS = 8
HEAD = 128
D = 2048
COLS = 64
ROWS = 4
HALO = 3
BLOCK = 16
SET = ROWS * COLS
KV_ROWS = (BLOCK + 2 * HALO) * COLS
FP_TOP = 448.0
AXES = ("y", "x", "z", "core")
GROUP = ("x", "core")
PEAK_ROWS = 16
KEYS = (ROWS + 2 * HALO) * COLS
OUTER, INNER = (0, 3), (1, 2)
NEG = -1e30


def device_of(y, x, z, core):
    return ((y * 4 + x) * 16 + z) * 2 + core


def head_permutations():
    main, extra = [], []
    for tile in range(16):
        m, odd = divmod(tile, 2)
        for shard in range(32):
            z, core = divmod(shard, 2)
            source = tile * 32 + shard
            cut = 10 if odd else 21
            first = 3 * m + odd

            def target(block):
                head = block % HEADS
                return device_of(2 * odd + core, head // 2, z, head % 2)

            main.append((source, target(first if shard <= cut else first + 1)))
            if shard == cut:
                extra.append((source, target(first + 1)))
    return main, extra


def column_order(head, y):
    d = lax.broadcasted_iota(jnp.int32, (3 * HEAD, 3 * HEAD), 1)
    r = lax.broadcasted_iota(jnp.int32, (3 * HEAD, 3 * HEAD), 0)
    natural = ((head + 2 * (d // HEAD)) % 3) * HEAD + d % HEAD
    half, m = natural // 192, natural % 192
    z, core, j = m // 12, (m % 12) // 6, m % 6
    away = (2 * half + core + 4 - y) % 4
    place = jnp.where(away == 3, 1, jnp.where(away == 0, 0, away + 1))
    return (place * 96 + z * 6 + j == r).astype(jnp.bfloat16)


def project_rows(scale_ref, x_ref, w_scr, qkv_ref, parts):
    scale = scale_ref[0]
    inverse = 1.0 / scale
    for place, part in enumerate(parts):
        tokens = x_ref[2 * part : 2 * part + 2].reshape(2 * SET, D)
        tokens = (tokens.astype(jnp.float32) * inverse).astype(jnp.bfloat16)
        tokens = jnp.clip(tokens, -FP_TOP, FP_TOP)
        out = lax.dot_general(
            tokens, w_scr[...], (((1,), (1,)), ((), ())), preferred_element_type=jnp.float32
        )
        out = (out * scale).astype(jnp.bfloat16).reshape(2, SET, 3 * HEAD)
        qkv_ref[2 * place : 2 * place + 2] = out


def project_outer_kernel(scale_ref, x_ref, w0_ref, w1_ref, w2_ref, w3_ref, order_ref, qkv_ref, top_ref, bottom_ref, w_ref, w_cat):
    for part, ref in enumerate((w0_ref, w1_ref, w2_ref, w3_ref)):
        w_cat[96 * part : 96 * (part + 1)] = ref[...]
    w_ref[...] = lax.dot_general(
        order_ref[...], w_cat[...], (((0,), (0,)), ((), ())), preferred_element_type=jnp.float32
    ).astype(jnp.bfloat16)
    project_rows(scale_ref, x_ref, w_ref, qkv_ref, OUTER)
    top_ref[...] = qkv_ref[:2, : HALO * COLS, HEAD:]
    bottom_ref[...] = qkv_ref[2:, SET - HALO * COLS :, HEAD:]


def project_inner_kernel(scale_ref, x_ref, w_ref, qkv_ref):
    project_rows(scale_ref, x_ref, w_ref, qkv_ref, INNER)


def project_outer(scale, tokens, weights, order):
    halo = jax.ShapeDtypeStruct((2, HALO * COLS, 2 * HEAD), jnp.bfloat16)
    vmem = pl.BlockSpec(memory_space=pltpu.VMEM)
    return pl.pallas_call(
        project_outer_kernel,
        out_shape=(
            jax.ShapeDtypeStruct((4, SET, 3 * HEAD), jnp.bfloat16),
            halo,
            halo,
            jax.ShapeDtypeStruct((3 * HEAD, D), jnp.bfloat16),
        ),
        in_specs=[pl.BlockSpec(memory_space=pltpu.SMEM)] + [vmem] * 6,
        out_specs=(vmem,) * 4,
        scratch_shapes=[pltpu.VMEM((3 * HEAD, D), jnp.bfloat16)],
        compiler_params=pltpu.CompilerParams(vmem_limit_bytes=24 * 2**20),
        cost_estimate=pl.CostEstimate(
            flops=2 * 4 * SET * D * 3 * HEAD, bytes_accessed=8 * 2**20, transcendentals=0
        ),
        name="project_outer",
    )(scale, tokens, *weights, order)


def project_inner(scale, tokens, weights):
    vmem = pl.BlockSpec(memory_space=pltpu.VMEM)
    return pl.pallas_call(
        project_inner_kernel,
        out_shape=jax.ShapeDtypeStruct((4, SET, 3 * HEAD), jnp.bfloat16),
        in_specs=[pl.BlockSpec(memory_space=pltpu.SMEM), vmem, vmem],
        out_specs=vmem,
        compiler_params=pltpu.CompilerParams(vmem_limit_bytes=24 * 2**20),
        cost_estimate=pl.CostEstimate(
            flops=2 * 4 * SET * D * 3 * HEAD, bytes_accessed=6 * 2**20, transcendentals=0
        ),
        name="project_inner",
    )(scale, tokens, weights)


def tile_column(outer_ref, inner_ref, part, image):
    ref, parts = (outer_ref, OUTER) if part in OUTER else (inner_ref, INNER)
    return ref.at[2 * parts.index(part) + image]


def attend_rows(units, place_ref, outer_ref, inner_ref, out_ref, kv):
    base = place_ref[0]
    scaling = float(HEAD) ** -0.5 * math.log2(math.e)
    shape = (SET, KEYS)
    q_row = lax.broadcasted_iota(jnp.int32, shape, 0)
    k_row = lax.broadcasted_iota(jnp.int32, shape, 1)
    row_step = k_row // COLS - q_row // COLS
    col_step = k_row % COLS - q_row % COLS
    window = (row_step >= 0) & (row_step <= 2 * HALO) & (col_step >= -HALO) & (col_step <= HALO)
    window = jnp.where(window, 0.0, NEG)
    centre = jnp.where((row_step == HALO) & (col_step == 0), 0.0, NEG)
    key_at = lax.broadcasted_iota(jnp.int32, (1, KEYS), 1)
    query_at = lax.broadcasted_iota(jnp.int32, (SET, 1), 0)
    highest = jnp.zeros((SET, HEAD), jnp.float32)
    for image in range(2):
        ext_rows, ext_cols = place_ref[1 + 2 * image], place_ref[2 + 2 * image]
        for unit in units:
            query = tile_column(outer_ref, inner_ref, unit, image)[:, :HEAD]
            start = unit * SET
            keys = kv[image, start : start + KEYS, :HEAD]
            values = kv[image, start : start + KEYS, HEAD:]
            scores = lax.dot_general(
                query, keys, (((1,), (1,)), ((), ())), preferred_element_type=jnp.float32
            )
            key_rows = base + (ROWS * unit - HALO) + key_at // COLS
            key_cols = key_at % COLS
            valid = (key_rows >= 0) & (key_rows < ext_rows) & (key_cols < ext_cols)
            bias = jnp.where(valid, window, centre)
            scores = scores * scaling + bias
            weights = jnp.exp2(scores - jnp.max(scores, axis=1, keepdims=True))
            weights = weights * (1.0 / jnp.sum(weights, axis=1, keepdims=True))
            result = jnp.dot(
                weights.astype(jnp.bfloat16), values, preferred_element_type=jnp.float32
            )
            inside = (base + ROWS * unit + query_at // COLS < ext_rows) & (query_at % COLS < ext_cols)
            result = jnp.where(inside, result, 0.0).astype(jnp.bfloat16)
            highest = jnp.maximum(highest, jnp.abs(result.astype(jnp.float32)))
            out_ref[2 * unit + image, :SET] = result
    return highest


def fill_keys(outer_ref, inner_ref, kv):
    for image in range(2):
        for part in range(4):
            start = HALO * COLS + part * SET
            kv[image, start : start + SET] = tile_column(outer_ref, inner_ref, part, image)[:, HEAD:]


def attend_inner_kernel(place_ref, outer_ref, inner_ref, out_ref, highest_ref, kv):
    fill_keys(outer_ref, inner_ref, kv)
    highest_ref[...] = attend_rows(INNER, place_ref, outer_ref, inner_ref, out_ref, kv)


def attend_outer_kernel(place_ref, peak_ref, outer_ref, inner_ref, above_ref, below_ref, done_ref, highest_ref, out_ref, kv):
    for image in range(2):
        kv[image, : HALO * COLS] = above_ref[image]
        kv[image, KV_ROWS - HALO * COLS :] = below_ref[image]
    fill_keys(outer_ref, inner_ref, kv)
    for group in range(2, 6):
        out_ref[group, :SET] = done_ref[group]
    highest = jnp.maximum(attend_rows(OUTER, place_ref, outer_ref, inner_ref, out_ref, kv), highest_ref[...])
    lines = lax.broadcasted_iota(jnp.int32, (PEAK_ROWS, HEAD), 0)
    peaks = jnp.where(lines < PEAK_ROWS // 2, peak_ref[0], jnp.max(highest)).astype(jnp.bfloat16)
    for group in range(8):
        out_ref[group, SET:, :] = peaks


def attend_inner(place, outer, inner):
    vmem = pl.BlockSpec(memory_space=pltpu.VMEM)
    return pl.pallas_call(
        attend_inner_kernel,
        out_shape=(
            jax.ShapeDtypeStruct((8, SET, HEAD), jnp.bfloat16),
            jax.ShapeDtypeStruct((SET, HEAD), jnp.float32),
        ),
        in_specs=[pl.BlockSpec(memory_space=pltpu.SMEM), vmem, vmem],
        out_specs=(vmem, vmem),
        scratch_shapes=[pltpu.VMEM((2, KV_ROWS, 2 * HEAD), jnp.bfloat16)],
        compiler_params=pltpu.CompilerParams(vmem_limit_bytes=24 * 2**20),
        cost_estimate=pl.CostEstimate(
            flops=4 * 4 * SET * KEYS * HEAD, bytes_accessed=2 * 2**20, transcendentals=4 * SET * KEYS
        ),
        name="attend_inner",
    )(place, outer, inner)


def attend_outer(place, peak_in, outer, inner, above, below, done, highest):
    vmem = pl.BlockSpec(memory_space=pltpu.VMEM)
    smem = pl.BlockSpec(memory_space=pltpu.SMEM)
    return pl.pallas_call(
        attend_outer_kernel,
        out_shape=jax.ShapeDtypeStruct((8, SET + PEAK_ROWS, HEAD), jnp.bfloat16),
        in_specs=[smem, smem] + [vmem] * 6,
        out_specs=vmem,
        scratch_shapes=[pltpu.VMEM((2, KV_ROWS, 2 * HEAD), jnp.bfloat16)],
        compiler_params=pltpu.CompilerParams(vmem_limit_bytes=24 * 2**20),
        cost_estimate=pl.CostEstimate(
            flops=4 * 4 * SET * KEYS * HEAD, bytes_accessed=3 * 2**20, transcendentals=4 * SET * KEYS
        ),
        name="attend_outer",
    )(place, peak_in, outer, inner, above, below, done, highest)


def spread(value, axis):
    size = math.prod(lax.axis_size(name) for name in ((axis,) if isinstance(axis, str) else axis))
    copies = jnp.broadcast_to(value[None], (size,) + value.shape)
    return lax.all_to_all(copies, axis, 0, 0, tiled=True)


def shift(value, axis, step):
    size = lax.axis_size(axis)
    return lax.ppermute(value, axis, [(i, (i + step) % size) for i in range(size)])


def head_weights(w_qkv, images):
    main, extra = head_permutations()
    mine = w_qkv.T
    first = lax.ppermute(mine, AXES, main)
    second = lax.ppermute(mine, AXES, extra)
    y, z = lax.axis_index("y"), lax.axis_index("z")
    shard = 2 * z + y % 2
    cut = jnp.where((y < 2) & (shard == 21), 2, jnp.where((y >= 2) & (shard == 10), 4, 6))
    column = lax.broadcasted_iota(jnp.int32, mine.shape, 0)
    merged = jnp.where(column < cut, first, second)
    with jax.named_scope("weights_over_z"):
        over_z = spread(merged.reshape(96, 128), "z").reshape(96, D)
    over_z, late = lax.optimization_barrier((over_z, images))
    with jax.named_scope("weights_over_y"):
        return [over_z] + [shift(over_z, "y", step) for step in (1, -1, 2)], late


def local(images, w_qkv, prev_scale, extent):
    with jax.named_scope("tokens"):
        tokens = lax.all_gather(images.reshape(SET, D), GROUP, axis=0, tiled=False)
    weights, late = head_weights(w_qkv, images)
    core = lax.axis_index("core")
    order = column_order(2 * lax.axis_index("x") + core, lax.axis_index("y"))
    other = shift(extent, "core", 1)
    peak_in = jnp.max(jnp.abs(late)).astype(jnp.float32).reshape(1)
    extents = jnp.where(core == 0, jnp.concatenate([extent, other]), jnp.concatenate([other, extent]))
    place = jnp.stack([lax.axis_index("y") * BLOCK, *extents.reshape(4)]).astype(jnp.int32)
    order, peak_in, place = lax.optimization_barrier((order, peak_in, place))
    outer, top, bottom, weights = project_outer(prev_scale, tokens, weights, order)
    with jax.named_scope("halo"):
        above = lax.ppermute(bottom, "y", [(i, i + 1) for i in range(3)])
        below = lax.ppermute(top, "y", [(i + 1, i) for i in range(3)])
    inner = project_inner(prev_scale, tokens, weights)
    done, highest = attend_inner(place, outer, inner)
    mixed = attend_outer(place, peak_in, outer, inner, above, below, done, highest)
    with jax.named_scope("heads"):
        mixed = lax.all_to_all(mixed, GROUP, 0, 0, tiled=True)
    attended = mixed[:, :SET].transpose(1, 0, 2).reshape(1, ROWS, COLS, HEADS * HEAD)
    peaks = mixed[:, SET:].astype(jnp.float32).reshape(8, 2, PEAK_ROWS // 2, HEAD)
    peaks = jnp.max(peaks, axis=(0, 2, 3))
    for axis in ("y", "z"):
        with jax.named_scope("peaks"):
            peaks = jnp.max(spread(peaks, axis).reshape(-1, 2), axis=0)
    return attended, peaks / FP_TOP


def solution(mesh):
    fine = Mesh(mesh.devices.reshape(4, 4, 16, 2), AXES)
    rows, columns = ("z", "core"), ("y", "x")
    return jax.shard_map(
        local,
        mesh=fine,
        in_specs=(P(rows, columns, None, None), P(None, AXES), P(), P(rows, None)),
        out_specs=(P(rows, columns, None, None), P()),
        check_vma=False,
    )
```

```python
import math

import jax
import jax.numpy as jnp
from jax import lax
from jax.experimental import pallas as pl
from jax.experimental.pallas import tpu as pltpu
from jax.sharding import Mesh
from jax.sharding import PartitionSpec as P

HEADS = 8
HEAD = 128
D = 2048
COLS = 64
ROWS = 4
HALO = 3
BLOCK = 16
SET = ROWS * COLS
KV_ROWS = (BLOCK + 2 * HALO) * COLS
FP_TOP = 448.0
AXES = ("y", "x", "z", "core")
GROUP = ("x", "core")
PEAK_ROWS = 16
KEYS = (ROWS + 2 * HALO) * COLS
OUTER, INNER = (0, 3), (1, 2)
NEG = -1e30


def device_of(y, x, z, core):
    return ((y * 4 + x) * 16 + z) * 2 + core


def head_permutations():
    main, extra = [], []
    for tile in range(16):
        m, odd = divmod(tile, 2)
        for shard in range(32):
            z, core = divmod(shard, 2)
            source = tile * 32 + shard
            cut = 10 if odd else 21
            first = 3 * m + odd

            def target(block):
                head = block % HEADS
                return device_of(2 * odd + core, head // 2, z, head % 2)

            main.append((source, target(first if shard <= cut else first + 1)))
            if shard == cut:
                extra.append((source, target(first + 1)))
    return main, extra


def column_order(head, y):
    d = lax.broadcasted_iota(jnp.int32, (3 * HEAD, 3 * HEAD), 1)
    r = lax.broadcasted_iota(jnp.int32, (3 * HEAD, 3 * HEAD), 0)
    natural = ((head + 2 * (d // HEAD)) % 3) * HEAD + d % HEAD
    half, m = natural // 192, natural % 192
    z, core, j = m // 12, (m % 12) // 6, m % 6
    away = (2 * half + core + 4 - y) % 4
    place = jnp.where(away == 3, 1, jnp.where(away == 0, 0, away + 1))
    return (place * 96 + z * 6 + j == r).astype(jnp.bfloat16)


def project_rows(scale_ref, x_refs, w_scr, qkv_ref):
    scale = scale_ref[0]
    inverse = 1.0 / scale
    for place, x_ref in enumerate(x_refs):
        tokens = x_ref[...].reshape(2 * SET, D)
        tokens = (tokens.astype(jnp.float32) * inverse).astype(jnp.bfloat16)
        tokens = jnp.clip(tokens, -FP_TOP, FP_TOP)
        out = lax.dot_general(
            tokens, w_scr[...], (((1,), (1,)), ((), ())), preferred_element_type=jnp.float32
        )
        out = (out * scale).astype(jnp.bfloat16).reshape(2, SET, 3 * HEAD)
        qkv_ref[2 * place : 2 * place + 2] = out


def project_outer_kernel(scale_ref, x0_ref, x3_ref, w0_ref, w1_ref, w2_ref, w3_ref, order_ref, qkv_ref, top_ref, bottom_ref, w_ref, w_cat):
    for part, ref in enumerate((w0_ref, w1_ref, w2_ref, w3_ref)):
        w_cat[96 * part : 96 * (part + 1)] = ref[...]
    w_ref[...] = lax.dot_general(
        order_ref[...], w_cat[...], (((0,), (0,)), ((), ())), preferred_element_type=jnp.float32
    ).astype(jnp.bfloat16)
    project_rows(scale_ref, (x0_ref, x3_ref), w_ref, qkv_ref)
    top_ref[...] = qkv_ref[:2, : HALO * COLS, HEAD:]
    bottom_ref[...] = qkv_ref[2:, SET - HALO * COLS :, HEAD:]


def project_inner_kernel(scale_ref, x1_ref, x2_ref, w_ref, qkv_ref):
    project_rows(scale_ref, (x1_ref, x2_ref), w_ref, qkv_ref)


def project_outer(scale, tokens, weights, order):
    halo = jax.ShapeDtypeStruct((2, HALO * COLS, 2 * HEAD), jnp.bfloat16)
    vmem = pl.BlockSpec(memory_space=pltpu.VMEM)
    return pl.pallas_call(
        project_outer_kernel,
        out_shape=(
            jax.ShapeDtypeStruct((4, SET, 3 * HEAD), jnp.bfloat16),
            halo,
            halo,
            jax.ShapeDtypeStruct((3 * HEAD, D), jnp.bfloat16),
        ),
        in_specs=[pl.BlockSpec(memory_space=pltpu.SMEM)] + [vmem] * 7,
        out_specs=(vmem,) * 4,
        scratch_shapes=[pltpu.VMEM((3 * HEAD, D), jnp.bfloat16)],
        compiler_params=pltpu.CompilerParams(vmem_limit_bytes=24 * 2**20),
        cost_estimate=pl.CostEstimate(
            flops=2 * 4 * SET * D * 3 * HEAD, bytes_accessed=8 * 2**20, transcendentals=0
        ),
        name="project_outer",
    )(scale, *tokens, *weights, order)


def project_inner(scale, tokens, weights):
    vmem = pl.BlockSpec(memory_space=pltpu.VMEM)
    return pl.pallas_call(
        project_inner_kernel,
        out_shape=jax.ShapeDtypeStruct((4, SET, 3 * HEAD), jnp.bfloat16),
        in_specs=[pl.BlockSpec(memory_space=pltpu.SMEM), vmem, vmem, vmem],
        out_specs=vmem,
        compiler_params=pltpu.CompilerParams(vmem_limit_bytes=24 * 2**20),
        cost_estimate=pl.CostEstimate(
            flops=2 * 4 * SET * D * 3 * HEAD, bytes_accessed=6 * 2**20, transcendentals=0
        ),
        name="project_inner",
    )(scale, *tokens, weights)


def tile_column(outer_ref, inner_ref, part, image):
    ref, parts = (outer_ref, OUTER) if part in OUTER else (inner_ref, INNER)
    return ref.at[2 * parts.index(part) + image]


def attend_rows(units, place_ref, outer_ref, inner_ref, out_ref, kv):
    base = place_ref[0]
    scaling = float(HEAD) ** -0.5 * math.log2(math.e)
    shape = (SET, KEYS)
    q_row = lax.broadcasted_iota(jnp.int32, shape, 0)
    k_row = lax.broadcasted_iota(jnp.int32, shape, 1)
    row_step = k_row // COLS - q_row // COLS
    col_step = k_row % COLS - q_row % COLS
    window = (row_step >= 0) & (row_step <= 2 * HALO) & (col_step >= -HALO) & (col_step <= HALO)
    window = jnp.where(window, 0.0, NEG)
    centre = jnp.where((row_step == HALO) & (col_step == 0), 0.0, NEG)
    key_at = lax.broadcasted_iota(jnp.int32, (1, KEYS), 1)
    query_at = lax.broadcasted_iota(jnp.int32, (SET, 1), 0)
    highest = jnp.zeros((SET, HEAD), jnp.float32)
    for image in range(2):
        ext_rows, ext_cols = place_ref[1 + 2 * image], place_ref[2 + 2 * image]
        for unit in units:
            query = tile_column(outer_ref, inner_ref, unit, image)[:, :HEAD]
            start = unit * SET
            keys = kv[image, start : start + KEYS, :HEAD]
            values = kv[image, start : start + KEYS, HEAD:]
            scores = lax.dot_general(
                query, keys, (((1,), (1,)), ((), ())), preferred_element_type=jnp.float32
            )
            key_rows = base + (ROWS * unit - HALO) + key_at // COLS
            key_cols = key_at % COLS
            valid = (key_rows >= 0) & (key_rows < ext_rows) & (key_cols < ext_cols)
            bias = jnp.where(valid, window, centre)
            scores = scores * scaling + bias
            weights = jnp.exp2(scores - jnp.max(scores, axis=1, keepdims=True))
            weights = weights * (1.0 / jnp.sum(weights, axis=1, keepdims=True))
            result = jnp.dot(
                weights.astype(jnp.bfloat16), values, preferred_element_type=jnp.float32
            )
            inside = (base + ROWS * unit + query_at // COLS < ext_rows) & (query_at % COLS < ext_cols)
            result = jnp.where(inside, result, 0.0).astype(jnp.bfloat16)
            highest = jnp.maximum(highest, jnp.abs(result.astype(jnp.float32)))
            out_ref[2 * unit + image, :SET] = result
    return highest


def fill_keys(outer_ref, inner_ref, kv):
    for image in range(2):
        for part in range(4):
            start = HALO * COLS + part * SET
            kv[image, start : start + SET] = tile_column(outer_ref, inner_ref, part, image)[:, HEAD:]


def attend_inner_kernel(place_ref, outer_ref, inner_ref, out_ref, highest_ref, kv):
    fill_keys(outer_ref, inner_ref, kv)
    highest_ref[...] = attend_rows(INNER, place_ref, outer_ref, inner_ref, out_ref, kv)


def attend_outer_kernel(place_ref, peak_ref, outer_ref, inner_ref, above_ref, below_ref, done_ref, highest_ref, out_ref, kv):
    for image in range(2):
        kv[image, : HALO * COLS] = above_ref[image]
        kv[image, KV_ROWS - HALO * COLS :] = below_ref[image]
    fill_keys(outer_ref, inner_ref, kv)
    for group in range(2, 6):
        out_ref[group, :SET] = done_ref[group]
    highest = jnp.maximum(attend_rows(OUTER, place_ref, outer_ref, inner_ref, out_ref, kv), highest_ref[...])
    lines = lax.broadcasted_iota(jnp.int32, (PEAK_ROWS, HEAD), 0)
    peaks = jnp.where(lines < PEAK_ROWS // 2, peak_ref[0], jnp.max(highest)).astype(jnp.bfloat16)
    for group in range(8):
        out_ref[group, SET:, :] = peaks


def attend_inner(place, outer, inner):
    vmem = pl.BlockSpec(memory_space=pltpu.VMEM)
    return pl.pallas_call(
        attend_inner_kernel,
        out_shape=(
            jax.ShapeDtypeStruct((8, SET, HEAD), jnp.bfloat16),
            jax.ShapeDtypeStruct((SET, HEAD), jnp.float32),
        ),
        in_specs=[pl.BlockSpec(memory_space=pltpu.SMEM), vmem, vmem],
        out_specs=(vmem, vmem),
        scratch_shapes=[pltpu.VMEM((2, KV_ROWS, 2 * HEAD), jnp.bfloat16)],
        compiler_params=pltpu.CompilerParams(vmem_limit_bytes=24 * 2**20),
        cost_estimate=pl.CostEstimate(
            flops=4 * 4 * SET * KEYS * HEAD, bytes_accessed=2 * 2**20, transcendentals=4 * SET * KEYS
        ),
        name="attend_inner",
    )(place, outer, inner)


def attend_outer(place, peak_in, outer, inner, above, below, done, highest):
    vmem = pl.BlockSpec(memory_space=pltpu.VMEM)
    smem = pl.BlockSpec(memory_space=pltpu.SMEM)
    return pl.pallas_call(
        attend_outer_kernel,
        out_shape=jax.ShapeDtypeStruct((8, SET + PEAK_ROWS, HEAD), jnp.bfloat16),
        in_specs=[smem, smem] + [vmem] * 6,
        out_specs=vmem,
        scratch_shapes=[pltpu.VMEM((2, KV_ROWS, 2 * HEAD), jnp.bfloat16)],
        compiler_params=pltpu.CompilerParams(vmem_limit_bytes=24 * 2**20),
        cost_estimate=pl.CostEstimate(
            flops=4 * 4 * SET * KEYS * HEAD, bytes_accessed=3 * 2**20, transcendentals=4 * SET * KEYS
        ),
        name="attend_outer",
    )(place, peak_in, outer, inner, above, below, done, highest)


def spread(value, axis):
    size = math.prod(lax.axis_size(name) for name in ((axis,) if isinstance(axis, str) else axis))
    copies = jnp.broadcast_to(value[None], (size,) + value.shape)
    return lax.all_to_all(copies, axis, 0, 0, tiled=True)


def shift(value, axis, step):
    size = lax.axis_size(axis)
    return lax.ppermute(value, axis, [(i, (i + step) % size) for i in range(size)])


def head_weights(w_qkv, images):
    main, extra = head_permutations()
    mine = w_qkv.T
    first = lax.ppermute(mine, AXES, main)
    second = lax.ppermute(mine, AXES, extra)
    y, z = lax.axis_index("y"), lax.axis_index("z")
    shard = 2 * z + y % 2
    cut = jnp.where((y < 2) & (shard == 21), 2, jnp.where((y >= 2) & (shard == 10), 4, 6))
    column = lax.broadcasted_iota(jnp.int32, mine.shape, 0)
    merged = jnp.where(column < cut, first, second)
    with jax.named_scope("weights_over_z"):
        over_z = spread(merged.reshape(96, 128), "z").reshape(96, D)
    over_z, late = lax.optimization_barrier((over_z, images))
    with jax.named_scope("weights_over_y"):
        return [over_z] + [shift(over_z, "y", step) for step in (1, -1, 2)], late


def local(images, w_qkv, prev_scale, extent):
    with jax.named_scope("tokens"):
        tokens = lax.all_gather(images.reshape(SET, D), GROUP, axis=0, tiled=False)
    tokens = [tokens[2 * part : 2 * part + 2] for part in range(4)]
    weights, late = head_weights(w_qkv, images)
    core = lax.axis_index("core")
    order = column_order(2 * lax.axis_index("x") + core, lax.axis_index("y"))
    other = shift(extent, "core", 1)
    peak_in = jnp.max(jnp.abs(late)).astype(jnp.float32).reshape(1)
    extents = jnp.where(core == 0, jnp.concatenate([extent, other]), jnp.concatenate([other, extent]))
    place = jnp.stack([lax.axis_index("y") * BLOCK, *extents.reshape(4)]).astype(jnp.int32)
    order, peak_in, place = lax.optimization_barrier((order, peak_in, place))
    outer, top, bottom, weights = project_outer(prev_scale, [tokens[part] for part in OUTER], weights, order)
    with jax.named_scope("halo"):
        above = lax.ppermute(bottom, "y", [(i, i + 1) for i in range(3)])
        below = lax.ppermute(top, "y", [(i + 1, i) for i in range(3)])
    inner = project_inner(prev_scale, [tokens[part] for part in INNER], weights)
    done, highest = attend_inner(place, outer, inner)
    mixed = attend_outer(place, peak_in, outer, inner, above, below, done, highest)
    with jax.named_scope("heads"):
        mixed = lax.all_to_all(mixed, GROUP, 0, 0, tiled=True)
    attended = mixed[:, :SET].transpose(1, 0, 2).reshape(1, ROWS, COLS, HEADS * HEAD)
    peaks = mixed[:, SET:].astype(jnp.float32).reshape(8, 2, PEAK_ROWS // 2, HEAD)
    peaks = jnp.max(peaks, axis=(0, 2, 3))
    for axis in ("y", "z"):
        with jax.named_scope("peaks"):
            peaks = jnp.max(spread(peaks, axis).reshape(-1, 2), axis=0)
    return attended, peaks / FP_TOP


def solution(mesh):
    fine = Mesh(mesh.devices.reshape(4, 4, 16, 2), AXES)
    rows, columns = ("z", "core"), ("y", "x")
    return jax.shard_map(
        local,
        mesh=fine,
        in_specs=(P(rows, columns, None, None), P(None, AXES), P(), P(rows, None)),
        out_specs=(P(rows, columns, None, None), P()),
        check_vma=False,
    )
```

```python
import math

import jax
import jax.numpy as jnp
from jax import lax
from jax.experimental import pallas as pl
from jax.experimental.pallas import tpu as pltpu
from jax.sharding import Mesh
from jax.sharding import PartitionSpec as P

HEADS = 8
HEAD = 128
D = 2048
COLS = 64
ROWS = 4
HALO = 3
BLOCK = 16
SET = ROWS * COLS
KV_ROWS = (BLOCK + 2 * HALO) * COLS
FP_TOP = 448.0
AXES = ("y", "x", "z", "core")
GROUP = ("x", "core")
PEAK_ROWS = 16
KEYS = (ROWS + 2 * HALO) * COLS
OUTER, INNER = (0, 3), (1, 2)
NEG = -1e30


def device_of(y, x, z, core):
    return ((y * 4 + x) * 16 + z) * 2 + core


def head_permutations():
    main, extra = [], []
    for tile in range(16):
        m, odd = divmod(tile, 2)
        for shard in range(32):
            z, core = divmod(shard, 2)
            source = tile * 32 + shard
            cut = 10 if odd else 21
            first = 3 * m + odd

            def target(block):
                head = block % HEADS
                return device_of(2 * odd + core, head // 2, z, head % 2)

            main.append((source, target(first if shard <= cut else first + 1)))
            if shard == cut:
                extra.append((source, target(first + 1)))
    return main, extra


def column_order(head, y):
    d = lax.broadcasted_iota(jnp.int32, (3 * HEAD, 3 * HEAD), 1)
    r = lax.broadcasted_iota(jnp.int32, (3 * HEAD, 3 * HEAD), 0)
    natural = ((head + 2 * (d // HEAD)) % 3) * HEAD + d % HEAD
    half, m = natural // 192, natural % 192
    z, core, j = m // 12, (m % 12) // 6, m % 6
    away = (2 * half + core + 4 - y) % 4
    place = jnp.where(away == 3, 1, jnp.where(away == 0, 0, away + 1))
    return (place * 96 + z * 6 + j == r).astype(jnp.bfloat16)


def project_rows(scale_ref, x_refs, w_scr, qkv_ref):
    scale = scale_ref[0]
    inverse = 1.0 / scale
    for place, x_ref in enumerate(x_refs):
        tokens = x_ref[...].reshape(2 * SET, D)
        tokens = (tokens.astype(jnp.float32) * inverse).astype(jnp.bfloat16)
        tokens = jnp.clip(tokens, -FP_TOP, FP_TOP)
        out = lax.dot_general(
            tokens, w_scr[...], (((1,), (1,)), ((), ())), preferred_element_type=jnp.float32
        )
        out = (out * scale).astype(jnp.bfloat16).reshape(2, SET, 3 * HEAD)
        qkv_ref[2 * place : 2 * place + 2] = out


def project_outer_kernel(scale_ref, x0_ref, x3_ref, w0_ref, w1_ref, w2_ref, w3_ref, order_ref, qkv_ref, top_ref, bottom_ref, w_ref, w_cat):
    for part, ref in enumerate((w0_ref, w1_ref, w2_ref, w3_ref)):
        w_cat[96 * part : 96 * (part + 1)] = ref[...]
    w_ref[...] = lax.dot_general(
        order_ref[...], w_cat[...], (((0,), (0,)), ((), ())), preferred_element_type=jnp.float32
    ).astype(jnp.bfloat16)
    project_rows(scale_ref, (x0_ref, x3_ref), w_ref, qkv_ref)
    top_ref[...] = qkv_ref[:2, : HALO * COLS, HEAD:]
    bottom_ref[...] = qkv_ref[2:, SET - HALO * COLS :, HEAD:]


def project_inner_kernel(scale_ref, x1_ref, x2_ref, w_ref, qkv_ref):
    project_rows(scale_ref, (x1_ref, x2_ref), w_ref, qkv_ref)


def project_outer(scale, tokens, weights, order):
    halo = jax.ShapeDtypeStruct((2, HALO * COLS, 2 * HEAD), jnp.bfloat16)
    vmem = pl.BlockSpec(memory_space=pltpu.VMEM)
    return pl.pallas_call(
        project_outer_kernel,
        out_shape=(
            jax.ShapeDtypeStruct((4, SET, 3 * HEAD), jnp.bfloat16),
            halo,
            halo,
            jax.ShapeDtypeStruct((3 * HEAD, D), jnp.bfloat16),
        ),
        in_specs=[pl.BlockSpec(memory_space=pltpu.SMEM)] + [vmem] * 7,
        out_specs=(vmem,) * 4,
        scratch_shapes=[pltpu.VMEM((3 * HEAD, D), jnp.bfloat16)],
        compiler_params=pltpu.CompilerParams(vmem_limit_bytes=24 * 2**20),
        cost_estimate=pl.CostEstimate(
            flops=2 * 4 * SET * D * 3 * HEAD, bytes_accessed=8 * 2**20, transcendentals=0
        ),
        name="project_outer",
    )(scale, *tokens, *weights, order)


def project_inner(scale, tokens, weights):
    vmem = pl.BlockSpec(memory_space=pltpu.VMEM)
    return pl.pallas_call(
        project_inner_kernel,
        out_shape=jax.ShapeDtypeStruct((4, SET, 3 * HEAD), jnp.bfloat16),
        in_specs=[pl.BlockSpec(memory_space=pltpu.SMEM), vmem, vmem, vmem],
        out_specs=vmem,
        compiler_params=pltpu.CompilerParams(vmem_limit_bytes=24 * 2**20),
        cost_estimate=pl.CostEstimate(
            flops=2 * 4 * SET * D * 3 * HEAD, bytes_accessed=6 * 2**20, transcendentals=0
        ),
        name="project_inner",
    )(scale, *tokens, weights)


def tile_column(outer_ref, inner_ref, part, image):
    ref, parts = (outer_ref, OUTER) if part in OUTER else (inner_ref, INNER)
    return ref.at[2 * parts.index(part) + image]


def attend_rows(units, place_ref, outer_ref, inner_ref, out_ref, kv):
    base = place_ref[0]
    scaling = float(HEAD) ** -0.5 * math.log2(math.e)
    shape = (SET, KEYS)
    q_row = lax.broadcasted_iota(jnp.int32, shape, 0)
    k_row = lax.broadcasted_iota(jnp.int32, shape, 1)
    row_step = k_row // COLS - q_row // COLS
    col_step = k_row % COLS - q_row % COLS
    window = (row_step >= 0) & (row_step <= 2 * HALO) & (col_step >= -HALO) & (col_step <= HALO)
    window = jnp.where(window, 0.0, NEG)
    centre = jnp.where((row_step == HALO) & (col_step == 0), 0.0, NEG)
    key_at = lax.broadcasted_iota(jnp.int32, (1, KEYS), 1)
    query_at = lax.broadcasted_iota(jnp.int32, (SET, 1), 0)
    highest = jnp.zeros((SET, HEAD), jnp.float32)
    for unit in units:
        start = unit * SET
        scores, weights = [], []
        for image in range(2):
            query = tile_column(outer_ref, inner_ref, unit, image)[:, :HEAD]
            keys = kv[image, start : start + KEYS, :HEAD]
            scores.append(
                lax.dot_general(query, keys, (((1,), (1,)), ((), ())), preferred_element_type=jnp.float32)
            )
        for image in range(2):
            ext_rows, ext_cols = place_ref[1 + 2 * image], place_ref[2 + 2 * image]
            key_rows = base + (ROWS * unit - HALO) + key_at // COLS
            key_cols = key_at % COLS
            valid = (key_rows >= 0) & (key_rows < ext_rows) & (key_cols < ext_cols)
            biased = scores[image] * scaling + jnp.where(valid, window, centre)
            part = jnp.exp2(biased - jnp.max(biased, axis=1, keepdims=True))
            part = part * (1.0 / jnp.sum(part, axis=1, keepdims=True))
            weights.append(part.astype(jnp.bfloat16))
        for image in range(2):
            ext_rows, ext_cols = place_ref[1 + 2 * image], place_ref[2 + 2 * image]
            values = kv[image, start : start + KEYS, HEAD:]
            result = jnp.dot(weights[image], values, preferred_element_type=jnp.float32)
            inside = (base + ROWS * unit + query_at // COLS < ext_rows) & (query_at % COLS < ext_cols)
            result = jnp.where(inside, result, 0.0).astype(jnp.bfloat16)
            highest = jnp.maximum(highest, jnp.abs(result.astype(jnp.float32)))
            out_ref[2 * unit + image, :SET] = result
    return highest


def fill_keys(outer_ref, inner_ref, kv):
    for image in range(2):
        for part in range(4):
            start = HALO * COLS + part * SET
            kv[image, start : start + SET] = tile_column(outer_ref, inner_ref, part, image)[:, HEAD:]


def attend_inner_kernel(place_ref, outer_ref, inner_ref, out_ref, highest_ref, kv):
    fill_keys(outer_ref, inner_ref, kv)
    highest_ref[...] = attend_rows(INNER, place_ref, outer_ref, inner_ref, out_ref, kv)


def attend_outer_kernel(place_ref, peak_ref, outer_ref, inner_ref, above_ref, below_ref, done_ref, highest_ref, out_ref, kv):
    for image in range(2):
        kv[image, : HALO * COLS] = above_ref[image]
        kv[image, KV_ROWS - HALO * COLS :] = below_ref[image]
    fill_keys(outer_ref, inner_ref, kv)
    for group in range(2, 6):
        out_ref[group, :SET] = done_ref[group]
    highest = jnp.maximum(attend_rows(OUTER, place_ref, outer_ref, inner_ref, out_ref, kv), highest_ref[...])
    lines = lax.broadcasted_iota(jnp.int32, (PEAK_ROWS, HEAD), 0)
    peaks = jnp.where(lines < PEAK_ROWS // 2, peak_ref[0], jnp.max(highest)).astype(jnp.bfloat16)
    for group in range(8):
        out_ref[group, SET:, :] = peaks


def attend_inner(place, outer, inner):
    vmem = pl.BlockSpec(memory_space=pltpu.VMEM)
    return pl.pallas_call(
        attend_inner_kernel,
        out_shape=(
            jax.ShapeDtypeStruct((8, SET, HEAD), jnp.bfloat16),
            jax.ShapeDtypeStruct((SET, HEAD), jnp.float32),
        ),
        in_specs=[pl.BlockSpec(memory_space=pltpu.SMEM), vmem, vmem],
        out_specs=(vmem, vmem),
        scratch_shapes=[pltpu.VMEM((2, KV_ROWS, 2 * HEAD), jnp.bfloat16)],
        compiler_params=pltpu.CompilerParams(vmem_limit_bytes=24 * 2**20),
        cost_estimate=pl.CostEstimate(
            flops=4 * 4 * SET * KEYS * HEAD, bytes_accessed=2 * 2**20, transcendentals=4 * SET * KEYS
        ),
        name="attend_inner",
    )(place, outer, inner)


def attend_outer(place, peak_in, outer, inner, above, below, done, highest):
    vmem = pl.BlockSpec(memory_space=pltpu.VMEM)
    smem = pl.BlockSpec(memory_space=pltpu.SMEM)
    return pl.pallas_call(
        attend_outer_kernel,
        out_shape=jax.ShapeDtypeStruct((8, SET + PEAK_ROWS, HEAD), jnp.bfloat16),
        in_specs=[smem, smem] + [vmem] * 6,
        out_specs=vmem,
        scratch_shapes=[pltpu.VMEM((2, KV_ROWS, 2 * HEAD), jnp.bfloat16)],
        compiler_params=pltpu.CompilerParams(vmem_limit_bytes=24 * 2**20),
        cost_estimate=pl.CostEstimate(
            flops=4 * 4 * SET * KEYS * HEAD, bytes_accessed=3 * 2**20, transcendentals=4 * SET * KEYS
        ),
        name="attend_outer",
    )(place, peak_in, outer, inner, above, below, done, highest)


def spread(value, axis):
    size = math.prod(lax.axis_size(name) for name in ((axis,) if isinstance(axis, str) else axis))
    copies = jnp.broadcast_to(value[None], (size,) + value.shape)
    return lax.all_to_all(copies, axis, 0, 0, tiled=True)


def shift(value, axis, step):
    size = lax.axis_size(axis)
    return lax.ppermute(value, axis, [(i, (i + step) % size) for i in range(size)])


def head_weights(w_qkv, images):
    main, extra = head_permutations()
    mine = w_qkv.T
    first = lax.ppermute(mine, AXES, main)
    second = lax.ppermute(mine, AXES, extra)
    y, z = lax.axis_index("y"), lax.axis_index("z")
    shard = 2 * z + y % 2
    cut = jnp.where((y < 2) & (shard == 21), 2, jnp.where((y >= 2) & (shard == 10), 4, 6))
    column = lax.broadcasted_iota(jnp.int32, mine.shape, 0)
    merged = jnp.where(column < cut, first, second)
    with jax.named_scope("weights_over_z"):
        over_z = spread(merged.reshape(96, 128), "z").reshape(96, D)
    over_z, late = lax.optimization_barrier((over_z, images))
    with jax.named_scope("weights_over_y"):
        return [over_z] + [shift(over_z, "y", step) for step in (1, -1, 2)], late


def local(images, w_qkv, prev_scale, extent):
    with jax.named_scope("tokens"):
        tokens = lax.all_gather(images.reshape(SET, D), GROUP, axis=0, tiled=False)
    tokens = [tokens[2 * part : 2 * part + 2] for part in range(4)]
    weights, late = head_weights(w_qkv, images)
    core = lax.axis_index("core")
    order = column_order(2 * lax.axis_index("x") + core, lax.axis_index("y"))
    other = shift(extent, "core", 1)
    peak_in = jnp.max(jnp.abs(late)).astype(jnp.float32).reshape(1)
    extents = jnp.where(core == 0, jnp.concatenate([extent, other]), jnp.concatenate([other, extent]))
    place = jnp.stack([lax.axis_index("y") * BLOCK, *extents.reshape(4)]).astype(jnp.int32)
    order, peak_in, place = lax.optimization_barrier((order, peak_in, place))
    outer, top, bottom, weights = project_outer(prev_scale, [tokens[part] for part in OUTER], weights, order)
    with jax.named_scope("halo"):
        above = lax.ppermute(bottom, "y", [(i, i + 1) for i in range(3)])
        below = lax.ppermute(top, "y", [(i + 1, i) for i in range(3)])
    inner = project_inner(prev_scale, [tokens[part] for part in INNER], weights)
    done, highest = attend_inner(place, outer, inner)
    mixed = attend_outer(place, peak_in, outer, inner, above, below, done, highest)
    with jax.named_scope("heads"):
        mixed = lax.all_to_all(mixed, GROUP, 0, 0, tiled=True)
    attended = mixed[:, :SET].transpose(1, 0, 2).reshape(1, ROWS, COLS, HEADS * HEAD)
    peaks = mixed[:, SET:].astype(jnp.float32).reshape(8, 2, PEAK_ROWS // 2, HEAD)
    peaks = jnp.max(peaks, axis=(0, 2, 3))
    for axis in ("y", "z"):
        with jax.named_scope("peaks"):
            peaks = jnp.max(spread(peaks, axis).reshape(-1, 2), axis=0)
    return attended, peaks / FP_TOP


def solution(mesh):
    fine = Mesh(mesh.devices.reshape(4, 4, 16, 2), AXES)
    rows, columns = ("z", "core"), ("y", "x")
    return jax.shard_map(
        local,
        mesh=fine,
        in_specs=(P(rows, columns, None, None), P(None, AXES), P(), P(rows, None)),
        out_specs=(P(rows, columns, None, None), P()),
        check_vma=False,
    )
```

```python
import math

import jax
import jax.numpy as jnp
from jax import lax
from jax.experimental import pallas as pl
from jax.experimental.pallas import tpu as pltpu
from jax.sharding import Mesh
from jax.sharding import PartitionSpec as P

HEADS = 8
HEAD = 128
D = 2048
COLS = 64
ROWS = 4
HALO = 3
BLOCK = 16
SET = ROWS * COLS
KV_ROWS = (BLOCK + 2 * HALO) * COLS
FP_TOP = 448.0
AXES = ("y", "x", "z", "core")
GROUP = ("x", "core")
PEAK_ROWS = 16
KEYS = (ROWS + 2 * HALO) * COLS
OUTER, INNER = (0, 3), (1, 2)
NEG = -1e30


def device_of(y, x, z, core):
    return ((y * 4 + x) * 16 + z) * 2 + core


def head_permutations():
    main, extra = [], []
    for tile in range(16):
        m, odd = divmod(tile, 2)
        for shard in range(32):
            z, core = divmod(shard, 2)
            source = tile * 32 + shard
            cut = 10 if odd else 21
            first = 3 * m + odd

            def target(block):
                head = block % HEADS
                return device_of(2 * odd + core, head // 2, z, head % 2)

            main.append((source, target(first if shard <= cut else first + 1)))
            if shard == cut:
                extra.append((source, target(first + 1)))
    return main, extra


def column_order(head, y):
    d = lax.broadcasted_iota(jnp.int32, (3 * HEAD, 3 * HEAD), 1)
    r = lax.broadcasted_iota(jnp.int32, (3 * HEAD, 3 * HEAD), 0)
    natural = ((head + 2 * (d // HEAD)) % 3) * HEAD + d % HEAD
    half, m = natural // 192, natural % 192
    z, core, j = m // 12, (m % 12) // 6, m % 6
    away = (2 * half + core + 4 - y) % 4
    place = jnp.where(away == 3, 1, jnp.where(away == 0, 0, away + 1))
    return (place * 96 + z * 6 + j == r).astype(jnp.bfloat16)


def project_rows(scale_ref, x_refs, w_scr, qkv_ref):
    scale = scale_ref[0]
    inverse = 1.0 / scale
    for place, x_ref in enumerate(x_refs):
        tokens = x_ref[...].reshape(2 * SET, D)
        tokens = (tokens.astype(jnp.float32) * inverse).astype(jnp.bfloat16)
        tokens = jnp.clip(tokens, -FP_TOP, FP_TOP)
        out = lax.dot_general(
            tokens, w_scr[...], (((1,), (1,)), ((), ())), preferred_element_type=jnp.float32
        )
        out = (out * scale).astype(jnp.bfloat16).reshape(2, SET, 3 * HEAD)
        qkv_ref[2 * place : 2 * place + 2] = out


def project_outer_kernel(scale_ref, x0_ref, x3_ref, w0_ref, w1_ref, w2_ref, w3_ref, order_ref, qkv_ref, top_ref, bottom_ref, w_ref, w_cat):
    for part, ref in enumerate((w0_ref, w1_ref, w2_ref, w3_ref)):
        w_cat[96 * part : 96 * (part + 1)] = ref[...]
    w_ref[...] = lax.dot_general(
        order_ref[...], w_cat[...], (((0,), (0,)), ((), ())), preferred_element_type=jnp.float32
    ).astype(jnp.bfloat16)
    project_rows(scale_ref, (x0_ref, x3_ref), w_ref, qkv_ref)
    top_ref[...] = qkv_ref[:2, : HALO * COLS, HEAD:]
    bottom_ref[...] = qkv_ref[2:, SET - HALO * COLS :, HEAD:]


def project_inner_kernel(scale_ref, x1_ref, x2_ref, w_ref, qkv_ref):
    project_rows(scale_ref, (x1_ref, x2_ref), w_ref, qkv_ref)


def project_outer(scale, tokens, weights, order):
    halo = jax.ShapeDtypeStruct((2, HALO * COLS, 2 * HEAD), jnp.bfloat16)
    vmem = pl.BlockSpec(memory_space=pltpu.VMEM)
    return pl.pallas_call(
        project_outer_kernel,
        out_shape=(
            jax.ShapeDtypeStruct((4, SET, 3 * HEAD), jnp.bfloat16),
            halo,
            halo,
            jax.ShapeDtypeStruct((3 * HEAD, D), jnp.bfloat16),
        ),
        in_specs=[pl.BlockSpec(memory_space=pltpu.SMEM)] + [vmem] * 7,
        out_specs=(vmem,) * 4,
        scratch_shapes=[pltpu.VMEM((3 * HEAD, D), jnp.bfloat16)],
        compiler_params=pltpu.CompilerParams(vmem_limit_bytes=24 * 2**20),
        cost_estimate=pl.CostEstimate(
            flops=2 * 4 * SET * D * 3 * HEAD, bytes_accessed=8 * 2**20, transcendentals=0
        ),
        name="project_outer",
    )(scale, *tokens, *weights, order)


def project_inner(scale, tokens, weights):
    vmem = pl.BlockSpec(memory_space=pltpu.VMEM)
    return pl.pallas_call(
        project_inner_kernel,
        out_shape=jax.ShapeDtypeStruct((4, SET, 3 * HEAD), jnp.bfloat16),
        in_specs=[pl.BlockSpec(memory_space=pltpu.SMEM), vmem, vmem, vmem],
        out_specs=vmem,
        compiler_params=pltpu.CompilerParams(vmem_limit_bytes=24 * 2**20),
        cost_estimate=pl.CostEstimate(
            flops=2 * 4 * SET * D * 3 * HEAD, bytes_accessed=6 * 2**20, transcendentals=0
        ),
        name="project_inner",
    )(scale, *tokens, weights)


def tile_column(outer_ref, inner_ref, part, image):
    ref, parts = (outer_ref, OUTER) if part in OUTER else (inner_ref, INNER)
    return ref.at[2 * parts.index(part) + image]


def attend_rows(units, place_ref, outer_ref, inner_ref, out_ref, kv):
    base = place_ref[0]
    scaling = float(HEAD) ** -0.5 * math.log2(math.e)
    shape = (SET, KEYS)
    q_row = lax.broadcasted_iota(jnp.int32, shape, 0)
    k_row = lax.broadcasted_iota(jnp.int32, shape, 1)
    row_step = k_row // COLS - q_row // COLS
    col_step = k_row % COLS - q_row % COLS
    window = (row_step >= 0) & (row_step <= 2 * HALO) & (col_step >= -HALO) & (col_step <= HALO)
    window = jnp.where(window, 0.0, NEG)
    centre = jnp.where((row_step == HALO) & (col_step == 0), 0.0, NEG)
    key_at = lax.broadcasted_iota(jnp.int32, (1, KEYS), 1)
    query_at = lax.broadcasted_iota(jnp.int32, (SET, 1), 0)
    highest = jnp.zeros((SET, HEAD), jnp.float32)
    for unit in units:
        start = unit * SET
        scores, weights = [], []
        for image in range(2):
            query = tile_column(outer_ref, inner_ref, unit, image)[:, :HEAD]
            keys = kv[image, start : start + KEYS, :HEAD]
            scores.append(
                lax.dot_general(query, keys, (((1,), (1,)), ((), ())), preferred_element_type=jnp.float32)
            )
        for image in range(2):
            ext_rows, ext_cols = place_ref[1 + 2 * image], place_ref[2 + 2 * image]
            key_rows = base + (ROWS * unit - HALO) + key_at // COLS
            key_cols = key_at % COLS
            valid = (key_rows >= 0) & (key_rows < ext_rows) & (key_cols < ext_cols)
            biased = scores[image] * scaling + jnp.where(valid, window, centre)
            part = jnp.exp2(biased - jnp.max(biased, axis=1, keepdims=True))
            part = part * (1.0 / jnp.sum(part, axis=1, keepdims=True))
            weights.append(part.astype(jnp.bfloat16))
        for image in range(2):
            ext_rows, ext_cols = place_ref[1 + 2 * image], place_ref[2 + 2 * image]
            values = kv[image, start : start + KEYS, HEAD:]
            result = jnp.dot(weights[image], values, preferred_element_type=jnp.float32)
            inside = (base + ROWS * unit + query_at // COLS < ext_rows) & (query_at % COLS < ext_cols)
            result = jnp.where(inside, result, 0.0).astype(jnp.bfloat16)
            highest = jnp.maximum(highest, jnp.abs(result.astype(jnp.float32)))
            out_ref[2 * unit + image, :SET] = result
    return highest


def fill_keys(outer_ref, inner_ref, kv):
    for image in range(2):
        for part in range(4):
            start = HALO * COLS + part * SET
            kv[image, start : start + SET] = tile_column(outer_ref, inner_ref, part, image)[:, HEAD:]


def attend_inner_kernel(place_ref, outer_ref, inner_ref, out_ref, highest_ref, kv):
    fill_keys(outer_ref, inner_ref, kv)
    highest_ref[...] = attend_rows(INNER, place_ref, outer_ref, inner_ref, out_ref, kv)


def attend_outer_kernel(place_ref, peak_ref, outer_ref, inner_ref, above_ref, below_ref, done_ref, highest_ref, out_ref, kv):
    for image in range(2):
        kv[image, : HALO * COLS] = above_ref[image]
        kv[image, KV_ROWS - HALO * COLS :] = below_ref[image]
    fill_keys(outer_ref, inner_ref, kv)
    for group in range(2, 6):
        out_ref[group, :SET] = done_ref[group]
    highest = jnp.maximum(attend_rows(OUTER, place_ref, outer_ref, inner_ref, out_ref, kv), highest_ref[...])
    lines = lax.broadcasted_iota(jnp.int32, (PEAK_ROWS, HEAD), 0)
    peaks = jnp.where(lines < PEAK_ROWS // 2, peak_ref[0], jnp.max(highest)).astype(jnp.bfloat16)
    for group in range(8):
        out_ref[group, SET:, :] = peaks


def attend_inner(place, outer, inner):
    vmem = pl.BlockSpec(memory_space=pltpu.VMEM)
    return pl.pallas_call(
        attend_inner_kernel,
        out_shape=(
            jax.ShapeDtypeStruct((8, SET, HEAD), jnp.bfloat16),
            jax.ShapeDtypeStruct((SET, HEAD), jnp.float32),
        ),
        in_specs=[pl.BlockSpec(memory_space=pltpu.SMEM), vmem, vmem],
        out_specs=(vmem, vmem),
        scratch_shapes=[pltpu.VMEM((2, KV_ROWS, 2 * HEAD), jnp.bfloat16)],
        compiler_params=pltpu.CompilerParams(vmem_limit_bytes=24 * 2**20),
        cost_estimate=pl.CostEstimate(
            flops=4 * 4 * SET * KEYS * HEAD, bytes_accessed=2 * 2**20, transcendentals=4 * SET * KEYS
        ),
        name="attend_inner",
    )(place, outer, inner)


def attend_outer(place, peak_in, outer, inner, above, below, done, highest):
    vmem = pl.BlockSpec(memory_space=pltpu.VMEM)
    smem = pl.BlockSpec(memory_space=pltpu.SMEM)
    return pl.pallas_call(
        attend_outer_kernel,
        out_shape=jax.ShapeDtypeStruct((8, SET + PEAK_ROWS, HEAD), jnp.bfloat16),
        in_specs=[smem, smem] + [vmem] * 6,
        out_specs=vmem,
        scratch_shapes=[pltpu.VMEM((2, KV_ROWS, 2 * HEAD), jnp.bfloat16)],
        compiler_params=pltpu.CompilerParams(vmem_limit_bytes=24 * 2**20),
        cost_estimate=pl.CostEstimate(
            flops=4 * 4 * SET * KEYS * HEAD, bytes_accessed=3 * 2**20, transcendentals=4 * SET * KEYS
        ),
        name="attend_outer",
    )(place, peak_in, outer, inner, above, below, done, highest)


def spread(value, axis):
    size = math.prod(lax.axis_size(name) for name in ((axis,) if isinstance(axis, str) else axis))
    copies = jnp.broadcast_to(value[None], (size,) + value.shape)
    return lax.all_to_all(copies, axis, 0, 0, tiled=True)


def shift(value, axis, step):
    size = lax.axis_size(axis)
    return lax.ppermute(value, axis, [(i, (i + step) % size) for i in range(size)])


def head_weights(w_qkv, images):
    main, extra = head_permutations()
    mine = w_qkv.T
    first = lax.ppermute(mine, AXES, main)
    second = lax.ppermute(mine, AXES, extra)
    y, z = lax.axis_index("y"), lax.axis_index("z")
    shard = 2 * z + y % 2
    cut = jnp.where((y < 2) & (shard == 21), 2, jnp.where((y >= 2) & (shard == 10), 4, 6))
    column = lax.broadcasted_iota(jnp.int32, mine.shape, 0)
    merged = jnp.where(column < cut, first, second)
    with jax.named_scope("weights_over_z"):
        over_z = spread(merged.reshape(96, 128), "z").reshape(96, D)
    over_z, late = lax.optimization_barrier((over_z, images))
    with jax.named_scope("weights_over_y"):
        return [over_z] + [shift(over_z, "y", step) for step in (1, -1, 2)], late


def local(images, w_qkv, prev_scale, extent):
    with jax.named_scope("tokens"):
        tokens = lax.all_gather(images.reshape(SET, D), GROUP, axis=0, tiled=False)
    weights, late = head_weights(w_qkv, images)
    core = lax.axis_index("core")
    order = column_order(2 * lax.axis_index("x") + core, lax.axis_index("y"))
    other = shift(extent, "core", 1)
    peak_in = jnp.max(jnp.abs(late)).astype(jnp.float32).reshape(1)
    extents = jnp.where(core == 0, jnp.concatenate([extent, other]), jnp.concatenate([other, extent]))
    place = jnp.stack([lax.axis_index("y") * BLOCK, *extents.reshape(4)]).astype(jnp.int32)
    order, peak_in, place = lax.optimization_barrier((order, peak_in, place))
    outer, top, bottom, weights = project_outer(prev_scale, [tokens[2 * part : 2 * part + 2] for part in OUTER], weights, order)
    with jax.named_scope("halo"):
        above = lax.ppermute(bottom, "y", [(i, i + 1) for i in range(3)])
        below = lax.ppermute(top, "y", [(i + 1, i) for i in range(3)])
    tokens = lax.optimization_barrier((tokens, weights))[0]
    inner = project_inner(prev_scale, [tokens[2 * part : 2 * part + 2] for part in INNER], weights)
    done, highest = attend_inner(place, outer, inner)
    mixed = attend_outer(place, peak_in, outer, inner, above, below, done, highest)
    with jax.named_scope("heads"):
        mixed = lax.all_to_all(mixed, GROUP, 0, 0, tiled=True)
    attended = mixed[:, :SET].transpose(1, 0, 2).reshape(1, ROWS, COLS, HEADS * HEAD)
    peaks = mixed[:, SET:].astype(jnp.float32).reshape(8, 2, PEAK_ROWS // 2, HEAD)
    peaks = jnp.max(peaks, axis=(0, 2, 3))
    for axis in ("y", "z"):
        with jax.named_scope("peaks"):
            peaks = jnp.max(spread(peaks, axis).reshape(-1, 2), axis=0)
    return attended, peaks / FP_TOP


def solution(mesh):
    fine = Mesh(mesh.devices.reshape(4, 4, 16, 2), AXES)
    rows, columns = ("z", "core"), ("y", "x")
    return jax.shard_map(
        local,
        mesh=fine,
        in_specs=(P(rows, columns, None, None), P(None, AXES), P(), P(rows, None)),
        out_specs=(P(rows, columns, None, None), P()),
        check_vma=False,
    )
```

```python
import math

import jax
import jax.numpy as jnp
from jax import lax
from jax.experimental import pallas as pl
from jax.experimental.pallas import tpu as pltpu
from jax.sharding import Mesh
from jax.sharding import PartitionSpec as P

HEADS = 8
HEAD = 128
D = 2048
COLS = 64
ROWS = 4
HALO = 3
BLOCK = 16
SET = ROWS * COLS
KV_ROWS = (BLOCK + 2 * HALO) * COLS
FP_TOP = 448.0
AXES = ("y", "x", "z", "core")
GROUP = ("x", "core")
PEAK_ROWS = 16
KEYS = (ROWS + 2 * HALO) * COLS
OUTER, INNER = (0, 3), (1, 2)
NEG = -1e30


def device_of(y, x, z, core):
    return ((y * 4 + x) * 16 + z) * 2 + core


def head_permutations():
    main, extra = [], []
    for tile in range(16):
        m, odd = divmod(tile, 2)
        for shard in range(32):
            z, core = divmod(shard, 2)
            source = tile * 32 + shard
            cut = 10 if odd else 21
            first = 3 * m + odd

            def target(block):
                head = block % HEADS
                return device_of(2 * odd + core, head // 2, z, head % 2)

            main.append((source, target(first if shard <= cut else first + 1)))
            if shard == cut:
                extra.append((source, target(first + 1)))
    return main, extra


def column_order(head, y):
    d = lax.broadcasted_iota(jnp.int32, (3 * HEAD, 3 * HEAD), 1)
    r = lax.broadcasted_iota(jnp.int32, (3 * HEAD, 3 * HEAD), 0)
    natural = ((head + 2 * (d // HEAD)) % 3) * HEAD + d % HEAD
    half, m = natural // 192, natural % 192
    z, core, j = m // 12, (m % 12) // 6, m % 6
    away = (2 * half + core + 4 - y) % 4
    place = jnp.where(away == 3, 1, jnp.where(away == 0, 0, away + 1))
    return (place * 96 + z * 6 + j == r).astype(jnp.bfloat16)


def project_rows(scale_ref, x_refs, w_scr, qkv_ref):
    scale = scale_ref[0]
    inverse = 1.0 / scale
    for place, x_ref in enumerate(x_refs):
        tokens = x_ref[...].reshape(2 * SET, D)
        tokens = (tokens.astype(jnp.float32) * inverse).astype(jnp.bfloat16)
        tokens = jnp.clip(tokens, -FP_TOP, FP_TOP)
        out = lax.dot_general(
            tokens, w_scr[...], (((1,), (1,)), ((), ())), preferred_element_type=jnp.float32
        )
        out = (out * scale).astype(jnp.bfloat16).reshape(2, SET, 3 * HEAD)
        qkv_ref[2 * place : 2 * place + 2] = out


def project_outer_kernel(scale_ref, x0_ref, x3_ref, w0_ref, w1_ref, w2_ref, w3_ref, order_ref, qkv_ref, top_ref, bottom_ref, w_ref):
    gathered = jnp.concatenate([ref[...] for ref in (w0_ref, w1_ref, w2_ref, w3_ref)])
    w_ref[...] = lax.dot_general(
        order_ref[...], gathered, (((0,), (0,)), ((), ())), preferred_element_type=jnp.float32
    ).astype(jnp.bfloat16)
    project_rows(scale_ref, (x0_ref, x3_ref), w_ref, qkv_ref)
    top_ref[...] = qkv_ref[:2, : HALO * COLS, HEAD:]
    bottom_ref[...] = qkv_ref[2:, SET - HALO * COLS :, HEAD:]


def project_inner_kernel(scale_ref, x1_ref, x2_ref, w_ref, qkv_ref):
    project_rows(scale_ref, (x1_ref, x2_ref), w_ref, qkv_ref)


def project_outer(scale, tokens, weights, order):
    halo = jax.ShapeDtypeStruct((2, HALO * COLS, 2 * HEAD), jnp.bfloat16)
    vmem = pl.BlockSpec(memory_space=pltpu.VMEM)
    return pl.pallas_call(
        project_outer_kernel,
        out_shape=(
            jax.ShapeDtypeStruct((4, SET, 3 * HEAD), jnp.bfloat16),
            halo,
            halo,
            jax.ShapeDtypeStruct((3 * HEAD, D), jnp.bfloat16),
        ),
        in_specs=[pl.BlockSpec(memory_space=pltpu.SMEM)] + [vmem] * 7,
        out_specs=(vmem,) * 4,
        compiler_params=pltpu.CompilerParams(vmem_limit_bytes=24 * 2**20),
        cost_estimate=pl.CostEstimate(
            flops=2 * 4 * SET * D * 3 * HEAD, bytes_accessed=8 * 2**20, transcendentals=0
        ),
        name="project_outer",
    )(scale, *tokens, *weights, order)


def project_inner(scale, tokens, weights):
    vmem = pl.BlockSpec(memory_space=pltpu.VMEM)
    return pl.pallas_call(
        project_inner_kernel,
        out_shape=jax.ShapeDtypeStruct((4, SET, 3 * HEAD), jnp.bfloat16),
        in_specs=[pl.BlockSpec(memory_space=pltpu.SMEM), vmem, vmem, vmem],
        out_specs=vmem,
        compiler_params=pltpu.CompilerParams(vmem_limit_bytes=24 * 2**20),
        cost_estimate=pl.CostEstimate(
            flops=2 * 4 * SET * D * 3 * HEAD, bytes_accessed=6 * 2**20, transcendentals=0
        ),
        name="project_inner",
    )(scale, *tokens, weights)


def tile_column(outer_ref, inner_ref, part, image):
    ref, parts = (outer_ref, OUTER) if part in OUTER else (inner_ref, INNER)
    return ref.at[2 * parts.index(part) + image]


def attend_rows(units, place_ref, outer_ref, inner_ref, out_ref, kv):
    base = place_ref[0]
    scaling = float(HEAD) ** -0.5 * math.log2(math.e)
    shape = (SET, KEYS)
    q_row = lax.broadcasted_iota(jnp.int32, shape, 0)
    k_row = lax.broadcasted_iota(jnp.int32, shape, 1)
    row_step = k_row // COLS - q_row // COLS
    col_step = k_row % COLS - q_row % COLS
    window = (row_step >= 0) & (row_step <= 2 * HALO) & (col_step >= -HALO) & (col_step <= HALO)
    window = jnp.where(window, 0.0, NEG)
    centre = jnp.where((row_step == HALO) & (col_step == 0), 0.0, NEG)
    key_at = lax.broadcasted_iota(jnp.int32, (1, KEYS), 1)
    query_at = lax.broadcasted_iota(jnp.int32, (SET, 1), 0)
    highest = jnp.zeros((SET, HEAD), jnp.float32)
    for unit in units:
        start = unit * SET
        scores, weights = [], []
        for image in range(2):
            query = tile_column(outer_ref, inner_ref, unit, image)[:, :HEAD]
            keys = kv[image, start : start + KEYS, :HEAD]
            scores.append(
                lax.dot_general(query, keys, (((1,), (1,)), ((), ())), preferred_element_type=jnp.float32)
            )
        for image in range(2):
            ext_rows, ext_cols = place_ref[1 + 2 * image], place_ref[2 + 2 * image]
            key_rows = base + (ROWS * unit - HALO) + key_at // COLS
            key_cols = key_at % COLS
            valid = (key_rows >= 0) & (key_rows < ext_rows) & (key_cols < ext_cols)
            biased = scores[image] * scaling + jnp.where(valid, window, centre)
            part = jnp.exp2(biased - jnp.max(biased, axis=1, keepdims=True))
            part = part * (1.0 / jnp.sum(part, axis=1, keepdims=True))
            weights.append(part.astype(jnp.bfloat16))
        for image in range(2):
            ext_rows, ext_cols = place_ref[1 + 2 * image], place_ref[2 + 2 * image]
            values = kv[image, start : start + KEYS, HEAD:]
            result = jnp.dot(weights[image], values, preferred_element_type=jnp.float32)
            inside = (base + ROWS * unit + query_at // COLS < ext_rows) & (query_at % COLS < ext_cols)
            result = jnp.where(inside, result, 0.0).astype(jnp.bfloat16)
            highest = jnp.maximum(highest, jnp.abs(result.astype(jnp.float32)))
            out_ref[2 * unit + image, :SET] = result
    return highest


def fill_keys(outer_ref, inner_ref, kv):
    for image in range(2):
        for part in range(4):
            start = HALO * COLS + part * SET
            kv[image, start : start + SET] = tile_column(outer_ref, inner_ref, part, image)[:, HEAD:]


def attend_inner_kernel(place_ref, outer_ref, inner_ref, out_ref, highest_ref, kv):
    fill_keys(outer_ref, inner_ref, kv)
    highest_ref[...] = attend_rows(INNER, place_ref, outer_ref, inner_ref, out_ref, kv)


def attend_outer_kernel(place_ref, peak_ref, outer_ref, inner_ref, above_ref, below_ref, done_ref, highest_ref, out_ref, kv):
    for image in range(2):
        kv[image, : HALO * COLS] = above_ref[image]
        kv[image, KV_ROWS - HALO * COLS :] = below_ref[image]
    fill_keys(outer_ref, inner_ref, kv)
    for group in range(2, 6):
        out_ref[group, :SET] = done_ref[group]
    highest = jnp.maximum(attend_rows(OUTER, place_ref, outer_ref, inner_ref, out_ref, kv), highest_ref[...])
    lines = lax.broadcasted_iota(jnp.int32, (PEAK_ROWS, HEAD), 0)
    peaks = jnp.where(lines < PEAK_ROWS // 2, peak_ref[0], jnp.max(highest)).astype(jnp.bfloat16)
    for group in range(8):
        out_ref[group, SET:, :] = peaks


def attend_inner(place, outer, inner):
    vmem = pl.BlockSpec(memory_space=pltpu.VMEM)
    return pl.pallas_call(
        attend_inner_kernel,
        out_shape=(
            jax.ShapeDtypeStruct((8, SET, HEAD), jnp.bfloat16),
            jax.ShapeDtypeStruct((SET, HEAD), jnp.float32),
        ),
        in_specs=[pl.BlockSpec(memory_space=pltpu.SMEM), vmem, vmem],
        out_specs=(vmem, vmem),
        scratch_shapes=[pltpu.VMEM((2, KV_ROWS, 2 * HEAD), jnp.bfloat16)],
        compiler_params=pltpu.CompilerParams(vmem_limit_bytes=24 * 2**20),
        cost_estimate=pl.CostEstimate(
            flops=4 * 4 * SET * KEYS * HEAD, bytes_accessed=2 * 2**20, transcendentals=4 * SET * KEYS
        ),
        name="attend_inner",
    )(place, outer, inner)


def attend_outer(place, peak_in, outer, inner, above, below, done, highest):
    vmem = pl.BlockSpec(memory_space=pltpu.VMEM)
    smem = pl.BlockSpec(memory_space=pltpu.SMEM)
    return pl.pallas_call(
        attend_outer_kernel,
        out_shape=jax.ShapeDtypeStruct((8, SET + PEAK_ROWS, HEAD), jnp.bfloat16),
        in_specs=[smem, smem] + [vmem] * 6,
        out_specs=vmem,
        scratch_shapes=[pltpu.VMEM((2, KV_ROWS, 2 * HEAD), jnp.bfloat16)],
        compiler_params=pltpu.CompilerParams(vmem_limit_bytes=24 * 2**20),
        cost_estimate=pl.CostEstimate(
            flops=4 * 4 * SET * KEYS * HEAD, bytes_accessed=3 * 2**20, transcendentals=4 * SET * KEYS
        ),
        name="attend_outer",
    )(place, peak_in, outer, inner, above, below, done, highest)


def spread(value, axis):
    size = math.prod(lax.axis_size(name) for name in ((axis,) if isinstance(axis, str) else axis))
    copies = jnp.broadcast_to(value[None], (size,) + value.shape)
    return lax.all_to_all(copies, axis, 0, 0, tiled=True)


def shift(value, axis, step):
    size = lax.axis_size(axis)
    return lax.ppermute(value, axis, [(i, (i + step) % size) for i in range(size)])


def head_weights(w_qkv, images):
    main, extra = head_permutations()
    mine = w_qkv.T
    first = lax.ppermute(mine, AXES, main)
    second = lax.ppermute(mine, AXES, extra)
    y, z = lax.axis_index("y"), lax.axis_index("z")
    shard = 2 * z + y % 2
    cut = jnp.where((y < 2) & (shard == 21), 2, jnp.where((y >= 2) & (shard == 10), 4, 6))
    column = lax.broadcasted_iota(jnp.int32, mine.shape, 0)
    merged = jnp.where(column < cut, first, second)
    with jax.named_scope("weights_over_z"):
        over_z = spread(merged.reshape(96, 128), "z").reshape(96, D)
    over_z, late = lax.optimization_barrier((over_z, images))
    with jax.named_scope("weights_over_y"):
        return [over_z] + [shift(over_z, "y", step) for step in (1, -1, 2)], late


def local(images, w_qkv, prev_scale, extent):
    with jax.named_scope("tokens"):
        tokens = lax.all_gather(images.reshape(SET, D), GROUP, axis=0, tiled=False)
    weights, late = head_weights(w_qkv, images)
    core = lax.axis_index("core")
    order = column_order(2 * lax.axis_index("x") + core, lax.axis_index("y"))
    other = shift(extent, "core", 1)
    peak_in = jnp.max(jnp.abs(late)).astype(jnp.float32).reshape(1)
    extents = jnp.where(core == 0, jnp.concatenate([extent, other]), jnp.concatenate([other, extent]))
    place = jnp.stack([lax.axis_index("y") * BLOCK, *extents.reshape(4)]).astype(jnp.int32)
    order, peak_in, place = lax.optimization_barrier((order, peak_in, place))
    outer, top, bottom, weights = project_outer(prev_scale, [tokens[2 * part : 2 * part + 2] for part in OUTER], weights, order)
    with jax.named_scope("halo"):
        above = lax.ppermute(bottom, "y", [(i, i + 1) for i in range(3)])
        below = lax.ppermute(top, "y", [(i + 1, i) for i in range(3)])
    tokens = lax.optimization_barrier((tokens, weights))[0]
    inner = project_inner(prev_scale, [tokens[2 * part : 2 * part + 2] for part in INNER], weights)
    done, highest = attend_inner(place, outer, inner)
    mixed = attend_outer(place, peak_in, outer, inner, above, below, done, highest)
    with jax.named_scope("heads"):
        mixed = lax.all_to_all(mixed, GROUP, 0, 0, tiled=True)
    attended = mixed[:, :SET].transpose(1, 0, 2).reshape(1, ROWS, COLS, HEADS * HEAD)
    peaks = mixed[:, SET:].astype(jnp.float32).reshape(8, 2, PEAK_ROWS // 2, HEAD)
    peaks = jnp.max(peaks, axis=(0, 2, 3))
    for axis in ("y", "z"):
        with jax.named_scope("peaks"):
            peaks = jnp.max(spread(peaks, axis).reshape(-1, 2), axis=0)
    return attended, peaks / FP_TOP


def solution(mesh):
    fine = Mesh(mesh.devices.reshape(4, 4, 16, 2), AXES)
    rows, columns = ("z", "core"), ("y", "x")
    return jax.shard_map(
        local,
        mesh=fine,
        in_specs=(P(rows, columns, None, None), P(None, AXES), P(), P(rows, None)),
        out_specs=(P(rows, columns, None, None), P()),
        check_vma=False,
    )
```
